128 devices in a mesh: cp: 64 (over z, y_lo, x, core), hd: 2 (over y_hi).
Axes of the slice: x: 4, y: 4 (y_hi: 2, y_lo: 2; y = y_hi * 2 + y_lo), z: 4, core: 2. Of those that a mesh axis runs over, the one named last changes fastest.
Arguments:
- query: bfloat16 [32768, 512], P('cp', 'hd'), may hold values from -6 to 6
- keys: bfloat16 [32768, 128], P('cp'), may hold values from -4 to 4
- values: bfloat16 [32768, 128], P('cp'), may hold values from -4 to 6
- grad_out: bfloat16 [32768, 512], P('cp', 'hd'), may hold values from -6 to 6
- doc_start: int32 [32768], P('cp'), may hold values from 0 to 32767, as said below
Outputs:
- grad_query: bfloat16 [32768, 512], P('cp', 'hd')
- grad_keys: bfloat16 [32768, 128], P('cp')
- grad_values: bfloat16 [32768, 128], P('cp')
The draws below stay inside these ranges and needn't reach their ends.
Inputs may be any that keep to these rules, and one draw needn't show every extreme that they name: `doc_start`: documents are contiguous runs of tokens of at most 4096 tokens; no document crosses a multiple of 4096 tokens; the first 4096 tokens form one document; the last token forms a document of its own.
All inputs are finite; a program needn't handle non-finite values.
Results may differ from the reference program's by a relative error of at most 0.0075.
Values may be sent and summed in bfloat16 or wider, within the bound.
No kernel may reach another device: no remote copies, remote signals or barrier semaphores. Data moves between devices by JAX's collectives and lax.ppermute only.
A program may use at most 64 MiB of HBM per device.

```python
import math
import jax
import jax.numpy as jnp
from jax import lax

HEADS = 4
HDIM = 128
TOK_DEV = 512
SPAN = 8
MAXDOC = 4096
TOKENS = 32768
N_CP = 64


def draw_query(key, part):
    key = jax.random.fold_in(key, 11)
    drawn = jnp.clip(jax.random.normal(key, (TOKENS, HEADS * HDIM), jnp.float32), -4.0, 4.0)
    return drawn.astype(jnp.bfloat16)


def draw_keys(key, part):
    key = jax.random.fold_in(key, 12)
    noise_key, scale_key = jax.random.split(key)
    block_scale = jnp.exp(jax.random.uniform(scale_key, (TOKENS // TOK_DEV,), jnp.float32, -0.7, 0.5))
    row_scale = block_scale[jnp.arange(TOKENS) // TOK_DEV]
    drawn = jnp.clip(jax.random.normal(noise_key, (TOKENS, HDIM), jnp.float32) * row_scale[:, None], -4.0, 4.0)
    return drawn.astype(jnp.bfloat16)


def draw_values(key, part):
    key = jax.random.fold_in(key, 14)
    noise_key, shift_key = jax.random.split(key)
    column_shift = jax.random.uniform(shift_key, (HDIM,), jnp.float32, 0.5, 1.5)
    noise = jnp.clip(jax.random.normal(noise_key, (TOKENS, HDIM), jnp.float32), -4.0, 4.0)
    return (noise + column_shift[None, :]).astype(jnp.bfloat16)


def draw_doc_start(key, part):
    key = jax.random.fold_in(key, 13)
    rate_key, token_key, forced_key = jax.random.split(key, 3)
    positions = jnp.arange(TOKENS, dtype=jnp.int32)
    block_index = positions // MAXDOC
    rate_bits = jax.random.randint(rate_key, (TOKENS // MAXDOC,), 3, 13)
    token_bits = rate_bits[block_index]
    tosses = jax.random.randint(token_key, (TOKENS,), 0, 4096)
    forced_pos = jax.random.randint(forced_key, (TOKENS // MAXDOC,), 1, MAXDOC)
    boundary = (tosses < 4096 >> token_bits) & (block_index > 0)
    boundary = boundary | (positions % MAXDOC == forced_pos[block_index]) & (block_index > 0)
    boundary = boundary | (positions % MAXDOC == 0) | (positions == TOKENS - 1)
    starts = jnp.where(boundary, positions, 0)
    return lax.cummax(starts, axis=0).astype(jnp.int32)


def steps_of(key, shape, shards, smallest, largest):
    level = 1.0
    for position, blocks in shards:
        draws = jax.random.uniform(jax.random.fold_in(jax.random.fold_in(key, 6), position), (blocks,), jnp.float32, smallest / len(shards), largest / len(shards))
        level = level * jnp.repeat(jnp.exp(draws), shape[position] // blocks).reshape((-1,) + (1,) * (len(shape) - 1 - position))
    return level


def normal_values(own_key, extent, deviation, bound, pieces=(), kind=jnp.bfloat16):
    factor_of = steps_of(own_key, extent, pieces, -0.22, 0.18) if pieces else 1.0
    entries = jax.random.normal(own_key, extent, jnp.float32) * deviation * factor_of
    return jnp.minimum(jnp.maximum(entries, -bound), bound).astype(kind)


def setup_inputs(seed: int = 0) -> dict:
    splits = jax.random.split(jax.random.key(seed), 6)
    query = draw_query(jax.random.fold_in(splits[5], 71), 0)
    keys = draw_keys(jax.random.fold_in(splits[5], 71), 0)
    values = draw_values(jax.random.fold_in(splits[5], 71), 0)
    grad_out = normal_values(splits[3], (TOKENS, HEADS * HDIM), 1.0, 6.0, ((0, 64), (1, 2)))
    doc_start = draw_doc_start(jax.random.fold_in(splits[5], 71), 0)
    return dict(query=query, keys=keys, values=values, grad_out=grad_out, doc_start=doc_start)


masked_score = -1e+30

def low_round(tensor):
    return lax.optimization_barrier(tensor.astype(jnp.bfloat16)).astype(jnp.float32)

def reference(query, keys, values, grad_out, doc_start):
    scaling = 1.0 / math.sqrt(HDIM)
    lookback = (SPAN - 1) * TOK_DEV
    window = SPAN * TOK_DEV
    query_heads = query.reshape(TOKENS, HEADS, HDIM)
    grad_heads = grad_out.reshape(TOKENS, HEADS, HDIM)
    keys_padded = jnp.concatenate([jnp.zeros((lookback, HDIM), keys.dtype), keys], 0)
    values_padded = jnp.concatenate([jnp.zeros((lookback, HDIM), values.dtype), values], 0)

    def one_block(carried, block):
        key_grad, value_grad = carried
        first = (block * TOK_DEV).astype(jnp.int32)
        query_part = lax.dynamic_slice_in_dim(query_heads, first, TOK_DEV, 0).astype(jnp.float32)
        grad_part = lax.dynamic_slice_in_dim(grad_heads, first, TOK_DEV, 0).astype(jnp.float32)
        key_part = lax.dynamic_slice_in_dim(keys_padded, first, window, 0).astype(jnp.float32)
        value_part = lax.dynamic_slice_in_dim(values_padded, first, window, 0).astype(jnp.float32)
        starts = lax.dynamic_slice_in_dim(doc_start, first, TOK_DEV, 0).astype(jnp.int32)
        query_pos = first + jnp.arange(TOK_DEV, dtype=jnp.int32)
        key_pos = first - lookback + jnp.arange(window, dtype=jnp.int32)
        allowed = (key_pos[None, :] >= starts[:, None]) & (key_pos[None, :] <= query_pos[:, None])
        scores = jnp.einsum('thd,kd->htk', query_part, key_part) * scaling
        scores = jnp.where(allowed[None], scores, masked_score)
        row_max = lax.optimization_barrier(jnp.max(scores, axis=-1, keepdims=True))
        log_norm = row_max + jnp.log(lax.optimization_barrier(jnp.sum(jnp.exp(scores - row_max), axis=-1, keepdims=True)))
        probs = jnp.where(allowed[None], jnp.exp(scores - log_norm), 0.0)
        grad_prob = jnp.einsum('thd,kd->htk', grad_part, value_part)
        row_delta = lax.optimization_barrier(jnp.sum(probs * grad_prob, axis=-1, keepdims=True))
        grad_score = low_round(probs * (grad_prob - row_delta))
        probs_low = low_round(probs)
        grad_query = (jnp.einsum('htk,kd->thd', grad_score, key_part) * scaling).astype(jnp.bfloat16)
        key_term = jnp.einsum('htk,thd->kd', grad_score, query_part) * scaling
        value_term = jnp.einsum('htk,thd->kd', probs_low, grad_part)
        key_grad = lax.dynamic_update_slice_in_dim(key_grad, lax.dynamic_slice_in_dim(key_grad, first, window, 0) + key_term, first, 0)
        value_grad = lax.dynamic_update_slice_in_dim(value_grad, lax.dynamic_slice_in_dim(value_grad, first, window, 0) + value_term, first, 0)
        return ((key_grad, value_grad), grad_query.reshape(TOK_DEV, HEADS * HDIM))
    start_grads = (jnp.zeros((TOKENS + lookback, HDIM), jnp.float32), jnp.zeros((TOKENS + lookback, HDIM), jnp.float32))
    (key_grad, value_grad), query_blocks = lax.scan(one_block, start_grads, jnp.arange(N_CP, dtype=jnp.int32))
    grad_query = query_blocks.reshape(TOKENS, HEADS * HDIM)
    grad_keys = key_grad[lookback:].astype(jnp.bfloat16)
    grad_values = value_grad[lookback:].astype(jnp.bfloat16)
    return (grad_query, grad_keys, grad_values)
```

```python
import functools
import math

import jax
import jax.numpy as jnp
from jax import lax
from jax.experimental import pallas as pl
from jax.experimental.pallas import tpu as pltpu
from jax.sharding import PartitionSpec as P

HDIM = 128
GROUP = 8
SCALE = 1.0 / math.sqrt(HDIM)
EXP_SCALE = SCALE * math.log2(math.e)
MASKED = -1e30
FLOOR = -1e29

NT = (((1,), (1,)), ((), ()))
NN = (((1,), (0,)), ((), ()))
TN = (((0,), (0,)), ((), ()))


def dot(a, b, dims):
    return lax.dot_general(a, b, dims, preferred_element_type=jnp.float32)


def chip_shift(array, by):
    n = lax.axis_size("cp")
    pairs = [(i, i - i % GROUP + (i % GROUP + 2 * by) % GROUP) for i in range(n)]
    return lax.ppermute(array, "cp", pairs)


def core_swap(array):
    n = lax.axis_size("cp")
    return lax.ppermute(array, "cp", [(i, i ^ 1) for i in range(n)])


def hd_swap(array):
    return lax.ppermute(array, "hd", [(0, 1), (1, 0)])


def masked_scores(k, q, starts, row_base, key_base, diagonal):
    s = dot(k, q, NT)
    key_pos = key_base + lax.broadcasted_iota(jnp.int32, s.shape, 0)
    allowed = key_pos >= starts
    if diagonal:
        row_pos = row_base + lax.broadcasted_iota(jnp.int32, s.shape, 1)
        allowed = allowed & (key_pos <= row_pos)
    return jnp.where(allowed, s, MASKED)


def stats_kernel(shifts, pos_ref, stats_in, *refs):
    kv_refs, (q_own, q_sib, g_own, g_sib, st_own, st_sib, stats) = refs[: len(shifts)], refs[len(shifts) :]
    cp = pos_ref[0]
    in_group = lax.rem(cp, GROUP)
    size = q_own.shape[0]
    stats[...] = stats_in[...]
    for kv, shift in zip(kv_refs, shifts):
        key_block = cp - 2 * shift
        for group, (q, g, st) in enumerate(((q_own, g_own, st_own), (q_sib, g_sib, st_sib))):
            row_block = cp if group == 0 else cp + 1 - 2 * lax.rem(cp, 2)

            def work(kv=kv, q=q, g=g, st=st, group=group, shift=shift, key_block=key_block, row_block=row_block):
                for head in range(2):
                    cols = pl.ds(head * HDIM, HDIM)
                    s = masked_scores(
                        kv[:, 0:HDIM], q[:, cols], st[...], row_block * size, key_block * size, shift == 0 and group == 0
                    )
                    dp = dot(kv[:, HDIM:], g[:, cols], NT)
                    at = 3 * (2 * group + head)
                    m = stats[at : at + 1, :]
                    new = jnp.maximum(m, jnp.max(s, axis=0, keepdims=True))
                    p = jnp.exp2((s - new) * EXP_SCALE)
                    f = jnp.exp2((m - new) * EXP_SCALE)
                    stats[at : at + 1, :] = new
                    stats[at + 1 : at + 2, :] = stats[at + 1 : at + 2, :] * f + jnp.sum(p, axis=0, keepdims=True)
                    stats[at + 2 : at + 3, :] = stats[at + 2 : at + 3, :] * f + jnp.sum(p * dp, axis=0, keepdims=True)

            if shift == 0 and group == 0:
                work()
            elif shift == 0:
                pl.when(lax.rem(cp, 2) == 0)(work)
            else:
                pl.when(in_group >= 2 * shift)(work)


def grads_kernel(shift, first, pos_ref, *refs):
    if first:
        kv, q_own, q_sib, g_own, g_sib, st_own, st_sib, fin, dq, dkv, acc = refs
        dq_in = None
    else:
        dq_in, kv, q_own, q_sib, g_own, g_sib, st_own, st_sib, fin, dq, dkv, acc = refs
    cp = pos_ref[0]
    in_group = lax.rem(cp, GROUP)
    size = q_own.shape[0]
    acc[...] = jnp.zeros_like(acc)
    if first:
        dq[...] = jnp.zeros_like(dq)
    else:
        dq[...] = dq_in[...]
    key_block = cp - 2 * shift
    for group, (q, g, st) in enumerate(((q_own, g_own, st_own), (q_sib, g_sib, st_sib))):
        row_block = cp if group == 0 else cp + 1 - 2 * lax.rem(cp, 2)

        def work(q=q, g=g, st=st, group=group, row_block=row_block):
            for head in range(2):
                cols = pl.ds(head * HDIM, HDIM)
                k = kv[:, 0:HDIM]
                s = masked_scores(k, q[:, cols], st[...], row_block * size, key_block * size, shift == 0 and group == 0)
                dp = dot(kv[:, HDIM:], g[:, cols], NT)
                at = 2 * (2 * group + head)
                p = jnp.exp2(s * EXP_SCALE - fin[at : at + 1, :])
                ds = (p * (dp - fin[at + 1 : at + 2, :])).astype(jnp.bfloat16)
                acc[:, 0:HDIM] += dot(ds, q[:, cols], NN)
                acc[:, HDIM:] += dot(p.astype(jnp.bfloat16), g[:, cols], NN)
                dq[group * size : (group + 1) * size, cols] += dot(ds, k, TN)

        if shift == 0 and group == 0:
            work()
        elif shift == 0:
            pl.when(lax.rem(cp, 2) == 0)(work)
        else:
            pl.when(in_group >= 2 * shift)(work)
    dkv[...] = acc[...].astype(dkv.dtype)


VM = pl.BlockSpec(memory_space=pltpu.VMEM)
SM = pl.BlockSpec(memory_space=pltpu.SMEM)


def call_stats(shifts, cp, stats, blocks, rows):
    units = 4 * len(shifts)
    return pl.pallas_call(
        functools.partial(stats_kernel, shifts),
        out_shape=jax.ShapeDtypeStruct(stats.shape, jnp.float32),
        in_specs=[SM] + [VM] * (1 + len(shifts) + len(rows)),
        out_specs=VM,
        compiler_params=pltpu.CompilerParams(vmem_limit_bytes=32 * 2**20),
        cost_estimate=pl.CostEstimate(flops=units * 4 * 512 * 512 * 128, bytes_accessed=2**20, transcendentals=units * 512 * 512),
        name="stats",
    )(cp, stats, *blocks, *rows)


def call_grads(shift, cp, dq, block, rows, fin):
    size = block.shape[0]
    first = dq is None
    out = (
        jax.ShapeDtypeStruct((2 * size, 2 * HDIM), jnp.float32),
        jax.ShapeDtypeStruct((size, 2 * HDIM), jnp.float32 if shift == 0 else jnp.bfloat16),
    )
    return pl.pallas_call(
        functools.partial(grads_kernel, shift, first),
        out_shape=out,
        in_specs=[SM] + [VM] * (2 + len(rows) + (0 if first else 1)),
        out_specs=(VM, VM),
        scratch_shapes=[pltpu.VMEM((size, 2 * HDIM), jnp.float32)],
        compiler_params=pltpu.CompilerParams(vmem_limit_bytes=32 * 2**20),
        cost_estimate=pl.CostEstimate(flops=4 * 10 * 512 * 512 * 128, bytes_accessed=3 * 2**20, transcendentals=4 * 512 * 512),
        name="grads",
    )(cp, *([] if first else [dq]), block, *rows, fin)


def body(query, keys, values, grad_out, doc_start):
    size = query.shape[0]
    position = lax.axis_index("cp").astype(jnp.int32)
    cp = position.reshape(1)
    kv = jnp.concatenate([keys, values], axis=1)
    from1 = chip_shift(kv, 1)
    from3 = chip_shift(kv, 3)
    from2 = chip_shift(kv, 2)
    starts = doc_start.reshape(1, size)
    rows = (query, core_swap(query), grad_out, core_swap(grad_out), starts, core_swap(starts))

    zero = jnp.zeros((4, 1, size), jnp.float32)
    stats = jnp.concatenate([zero + FLOOR, zero, zero], axis=1).reshape(12, size)
    stats = call_stats((0,), cp, stats, (kv,), rows)
    stats = call_stats((1, 3), cp, stats, (from1, from3), rows)
    stats = call_stats((2,), cp, stats, (from2,), rows)

    other = core_swap(stats).reshape(2, 6, size)[::-1].reshape(4, 3, size)
    mine = stats.reshape(4, 3, size)
    top = jnp.maximum(mine[:, 0], other[:, 0])
    f_mine = jnp.exp2((mine[:, 0] - top) * EXP_SCALE)
    f_other = jnp.exp2((other[:, 0] - top) * EXP_SCALE)
    total = mine[:, 1] * f_mine + other[:, 1] * f_other
    weighted = mine[:, 2] * f_mine + other[:, 2] * f_other
    fin = jnp.stack([top * EXP_SCALE + jnp.log2(total), weighted / total], axis=1).reshape(8, size)

    dq, part2 = call_grads(2, cp, None, from2, rows, fin)
    back2 = chip_shift(part2, 2)
    dq, part1 = call_grads(1, cp, dq, from1, rows, fin)
    back1 = chip_shift(part1, 3)
    dq, part3 = call_grads(3, cp, dq, from3, rows, fin)
    back3 = chip_shift(part3, 1)
    dq, own = call_grads(0, cp, dq, kv, rows, fin)

    dq_other = core_swap(dq[size:])
    grad_query = ((dq[:size] + dq_other) * SCALE).astype(jnp.bfloat16)

    f32 = jnp.float32
    half = (own + back1.astype(f32) + back3.astype(f32) + back2.astype(f32)).astype(jnp.bfloat16)
    dkv = half.astype(f32) + hd_swap(half).astype(f32)
    return (
        grad_query,
        (dkv[:, :HDIM] * SCALE).astype(jnp.bfloat16),
        dkv[:, HDIM:].astype(jnp.bfloat16),
    )


def solution(mesh):
    in_specs = (P("cp", "hd"), P("cp", None), P("cp", None), P("cp", "hd"), P("cp"))
    out_specs = (P("cp", "hd"), P("cp", None), P("cp", None))
    return jax.shard_map(body, mesh=mesh, in_specs=in_specs, out_specs=out_specs, check_vma=False)
```

```python
import functools
import math

import jax
import jax.numpy as jnp
from jax import lax
from jax.experimental import pallas as pl
from jax.experimental.pallas import tpu as pltpu
from jax.sharding import PartitionSpec as P

HDIM = 128
GROUP = 8
SCALE = 1.0 / math.sqrt(HDIM)
EXP_SCALE = SCALE * math.log2(math.e)
MASKED = -1e30
FLOOR = -1e29

NT = (((1,), (1,)), ((), ()))
NN = (((1,), (0,)), ((), ()))
TN = (((0,), (0,)), ((), ()))


def dot(a, b, dims):
    return lax.dot_general(a, b, dims, preferred_element_type=jnp.float32)


def chip_shift(array, by):
    n = lax.axis_size("cp")
    pairs = [(i, i - i % GROUP + (i % GROUP + 2 * by) % GROUP) for i in range(n)]
    return lax.ppermute(array, "cp", pairs)


def core_swap(array):
    n = lax.axis_size("cp")
    return lax.ppermute(array, "cp", [(i, i ^ 1) for i in range(n)])


def hd_swap(array):
    return lax.ppermute(array, "hd", [(0, 1), (1, 0)])


def masked_scores(k, q, starts, row_base, key_base, diagonal):
    s = dot(k, q, NT)
    key_pos = key_base + lax.broadcasted_iota(jnp.int32, s.shape, 0)
    allowed = key_pos >= starts
    if diagonal:
        row_pos = row_base + lax.broadcasted_iota(jnp.int32, s.shape, 1)
        allowed = allowed & (key_pos <= row_pos)
    return jnp.where(allowed, s, MASKED)


def stats_kernel(shifts, pos_ref, stats_in, *refs):
    kv_refs, (q_own, q_sib, g_own, g_sib, st_own, st_sib, stats) = refs[: len(shifts)], refs[len(shifts) :]
    cp = pos_ref[0]
    in_group = lax.rem(cp, GROUP)
    size = q_own.shape[0]
    stats[...] = stats_in[...]
    for kv, shift in zip(kv_refs, shifts):
        key_block = cp - 2 * shift
        for group, (q, g, st) in enumerate(((q_own, g_own, st_own), (q_sib, g_sib, st_sib))):
            row_block = cp if group == 0 else cp + 1 - 2 * lax.rem(cp, 2)

            def work(kv=kv, q=q, g=g, st=st, group=group, shift=shift, key_block=key_block, row_block=row_block):
                for head in range(2):
                    cols = pl.ds(head * HDIM, HDIM)
                    s = masked_scores(
                        kv[:, 0:HDIM], q[:, cols], st[...], row_block * size, key_block * size, shift == 0 and group == 0
                    )
                    dp = dot(kv[:, HDIM:], g[:, cols], NT)
                    at = 3 * (2 * group + head)
                    m = stats[at : at + 1, :]
                    new = jnp.maximum(m, jnp.max(s, axis=0, keepdims=True))
                    p = jnp.exp2((s - new) * EXP_SCALE)
                    f = jnp.exp2((m - new) * EXP_SCALE)
                    stats[at : at + 1, :] = new
                    stats[at + 1 : at + 2, :] = stats[at + 1 : at + 2, :] * f + jnp.sum(p, axis=0, keepdims=True)
                    stats[at + 2 : at + 3, :] = stats[at + 2 : at + 3, :] * f + jnp.sum(p * dp, axis=0, keepdims=True)

            if shift == 0 and group == 0:
                work()
            elif shift == 0:
                pl.when(lax.rem(cp, 2) == 0)(work)
            else:
                pl.when(in_group >= 2 * shift)(work)


def merged(stats, other, at, other_at):
    m, m2 = stats[at : at + 1, :], other[other_at : other_at + 1, :]
    top = jnp.maximum(m, m2)
    f, f2 = jnp.exp2((m - top) * EXP_SCALE), jnp.exp2((m2 - top) * EXP_SCALE)
    total = stats[at + 1 : at + 2, :] * f + other[other_at + 1 : other_at + 2, :] * f2
    weighted = stats[at + 2 : at + 3, :] * f + other[other_at + 2 : other_at + 3, :] * f2
    return top * EXP_SCALE + jnp.log2(total), weighted / total


def grads_kernel(shift, first, pos_ref, *refs):
    if first:
        stats, other, kv, q_own, q_sib, g_own, g_sib, st_own, st_sib, dq, dkv, fin, acc = refs
        for s in range(4):
            log_sum, delta = merged(stats, other, 3 * s, 3 * (s ^ 2))
            fin[2 * s : 2 * s + 1, :] = log_sum
            fin[2 * s + 1 : 2 * s + 2, :] = delta
        dq[...] = jnp.zeros_like(dq)
    else:
        dq_in, fin, kv, q_own, q_sib, g_own, g_sib, st_own, st_sib, dq, dkv, acc = refs
        dq[...] = dq_in[...]
    cp = pos_ref[0]
    in_group = lax.rem(cp, GROUP)
    size = q_own.shape[0]
    acc[...] = jnp.zeros_like(acc)
    key_block = cp - 2 * shift
    k_t = kv[:, 0:HDIM].T
    for group, (q, g, st) in enumerate(((q_own, g_own, st_own), (q_sib, g_sib, st_sib))):
        row_block = cp if group == 0 else cp + 1 - 2 * lax.rem(cp, 2)

        def work(q=q, g=g, st=st, group=group, row_block=row_block):
            for head in range(2):
                cols = pl.ds(head * HDIM, HDIM)
                k = kv[:, 0:HDIM]
                s = masked_scores(k, q[:, cols], st[...], row_block * size, key_block * size, shift == 0 and group == 0)
                dp = dot(kv[:, HDIM:], g[:, cols], NT)
                at = 2 * (2 * group + head)
                p = jnp.exp2(s * EXP_SCALE - fin[at : at + 1, :])
                ds = (p * (dp - fin[at + 1 : at + 2, :])).astype(jnp.bfloat16)
                acc[:, 0:HDIM] += dot(ds, q[:, cols], NN)
                acc[:, HDIM:] += dot(p.astype(jnp.bfloat16), g[:, cols], NN)
                dq[group, cols, :] += dot(k_t, ds, NN)

        if shift == 0 and group == 0:
            work()
        elif shift == 0:
            pl.when(lax.rem(cp, 2) == 0)(work)
        else:
            pl.when(in_group >= 2 * shift)(work)
    dkv[...] = acc[...].astype(dkv.dtype)


def pack_kernel(keys, values, kv):
    kv[:, 0:HDIM] = keys[...]
    kv[:, HDIM:] = values[...]


def query_kernel(mine, other, out):
    out[...] = ((mine[0] + other[...]) * SCALE).T.astype(out.dtype)


def add_kernel(total, part, out):
    out[...] = (total[...] + part[...].astype(jnp.float32)).astype(out.dtype)


def last_kernel(mine, other, grad_keys, grad_values):
    total = mine[...].astype(jnp.float32) + other[...].astype(jnp.float32)
    grad_keys[...] = (total[:, 0:HDIM] * SCALE).astype(grad_keys.dtype)
    grad_values[...] = total[:, HDIM:].astype(grad_values.dtype)


VM = pl.BlockSpec(memory_space=pltpu.VMEM)
SM = pl.BlockSpec(memory_space=pltpu.SMEM)


BLOCK_COST = pl.CostEstimate(flops=4 * 10 * 512 * 512 * 128, bytes_accessed=2**20, transcendentals=0)
NO_COST = pl.CostEstimate(flops=0, bytes_accessed=2**10, transcendentals=0)


def simple(kernel, out, *args, cost=NO_COST):
    return pl.pallas_call(
        kernel,
        out_shape=out,
        in_specs=[VM] * len(args),
        out_specs=jax.tree.map(lambda _: VM, out),
        cost_estimate=cost,
    )(*args)


def call_stats(shifts, cp, stats, blocks, rows):
    return pl.pallas_call(
        functools.partial(stats_kernel, shifts),
        out_shape=jax.ShapeDtypeStruct(stats.shape, jnp.float32),
        in_specs=[SM] + [VM] * (1 + len(shifts) + len(rows)),
        out_specs=VM,
        compiler_params=pltpu.CompilerParams(vmem_limit_bytes=32 * 2**20),
        cost_estimate=BLOCK_COST,
        name="stats",
    )(cp, stats, *blocks, *rows)


def call_grads(shift, cp, before, block, rows):
    size = block.shape[0]
    first = shift == 2
    out = [
        jax.ShapeDtypeStruct((2, 2 * HDIM, size), jnp.float32),
        jax.ShapeDtypeStruct((size, 2 * HDIM), jnp.float32 if shift == 0 else jnp.bfloat16),
    ]
    if first:
        out.append(jax.ShapeDtypeStruct((8, size), jnp.float32))
    return pl.pallas_call(
        functools.partial(grads_kernel, shift, first),
        out_shape=out,
        in_specs=[SM] + [VM] * (3 + len(rows)),
        out_specs=[VM] * len(out),
        scratch_shapes=[pltpu.VMEM((size, 2 * HDIM), jnp.float32)],
        compiler_params=pltpu.CompilerParams(vmem_limit_bytes=32 * 2**20),
        cost_estimate=NO_COST if shift == 0 else BLOCK_COST,
        name="grads",
    )(cp, *before, block, *rows)


def body(query, keys, values, grad_out, doc_start):
    size = query.shape[0]
    position = lax.axis_index("cp").astype(jnp.int32)
    cp = position.reshape(1)
    packed = jax.ShapeDtypeStruct((size, 2 * HDIM), jnp.bfloat16)
    kv = simple(pack_kernel, packed, keys, values)
    from1 = chip_shift(kv, 1)
    from3 = chip_shift(kv, 3)
    from2 = chip_shift(kv, 2)
    starts = doc_start.reshape(1, size)
    rows = (query, core_swap(query), grad_out, core_swap(grad_out), starts, core_swap(starts))

    zero = jnp.zeros((4, 1, size), jnp.float32)
    stats = jnp.concatenate([zero + FLOOR, zero, zero], axis=1).reshape(12, size)
    stats = call_stats((0,), cp, stats, (kv,), rows)
    stats = call_stats((1, 3), cp, stats, (from1, from3), rows)
    stats = call_stats((2,), cp, stats, (from2,), rows)

    dq, part2, fin = call_grads(2, cp, (stats, core_swap(stats)), from2, rows)
    back2 = chip_shift(part2, 2)
    dq, part1 = call_grads(1, cp, (dq, fin), from1, rows)
    back1 = chip_shift(part1, 3)
    dq, part3 = call_grads(3, cp, (dq, fin), from3, rows)
    back3 = chip_shift(part3, 1)
    dq, own = call_grads(0, cp, (dq, fin), kv, rows)

    dq_other = core_swap(dq[1])
    grad_query = simple(query_kernel, jax.ShapeDtypeStruct(query.shape, query.dtype), dq, dq_other)
    total = jax.ShapeDtypeStruct(own.shape, own.dtype)
    half = simple(add_kernel, total, own, back2, cost=BLOCK_COST)
    half = simple(add_kernel, total, half, back1, cost=BLOCK_COST)
    half = simple(add_kernel, packed, half, back3)
    other = hd_swap(half)
    grad_keys, grad_values = simple(last_kernel, [jax.ShapeDtypeStruct(keys.shape, keys.dtype)] * 2, half, other)
    return grad_query, grad_keys, grad_values


def solution(mesh):
    in_specs = (P("cp", "hd"), P("cp", None), P("cp", None), P("cp", "hd"), P("cp"))
    out_specs = (P("cp", "hd"), P("cp", None), P("cp", None))
    return jax.shard_map(body, mesh=mesh, in_specs=in_specs, out_specs=out_specs, check_vma=False)
```

```python
import functools
import math

import jax
import jax.numpy as jnp
from jax import lax
from jax.experimental import pallas as pl
from jax.experimental.pallas import tpu as pltpu
from jax.sharding import PartitionSpec as P

HDIM = 128
GROUP = 8
SCALE = 1.0 / math.sqrt(HDIM)
EXP_SCALE = SCALE * math.log2(math.e)
MASKED = -1e30
FLOOR = -1e29
KERNEL_VMEM = 16 * 2**20

NT = (((1,), (1,)), ((), ()))
NN = (((1,), (0,)), ((), ()))
TN = (((0,), (0,)), ((), ()))


def dot(a, b, dims):
    return lax.dot_general(a, b, dims, preferred_element_type=jnp.float32)


def chip_shift(array, even, odd):
    n = lax.axis_size("cp")
    pairs = [(i, i - i % GROUP + (i % GROUP + 2 * (odd if i % 2 else even)) % GROUP) for i in range(n)]
    return lax.ppermute(array, "cp", pairs)


def core_swap(array):
    n = lax.axis_size("cp")
    return lax.ppermute(array, "cp", [(i, i ^ 1) for i in range(n)])


def hd_swap(array):
    return lax.ppermute(array, "hd", [(0, 1), (1, 0)])


def masked_scores(k, q, starts, row_base, key_base, diagonal):
    s = dot(k, q, NT)
    key_pos = key_base + lax.broadcasted_iota(jnp.int32, s.shape, 0)
    allowed = key_pos >= starts
    if diagonal:
        row_pos = row_base + lax.broadcasted_iota(jnp.int32, s.shape, 1)
        allowed = allowed & (key_pos <= row_pos)
    return jnp.where(allowed, s, MASKED)


def distance(slot, cp):
    return slot if slot < 2 else slot + lax.rem(cp, 2) * (5 - 2 * slot)


def stats_kernel(shifts, pos_ref, *refs):
    n = len(shifts)
    first = shifts[0] == 0
    if not first:
        stats_in, *refs = refs
    blocks, (q_own, q_sib, g_own, g_sib, st_own, st_sib), outs = refs[:n], refs[n : n + 6], refs[n + 6 :]
    stats, kept = outs[0], outs[1:]
    cp = pos_ref[0]
    in_group = lax.rem(cp, GROUP)
    size = q_own.shape[0]
    if first:
        for at in range(0, 12, 3):
            stats[at : at + 1, :] = jnp.full((1, size), FLOOR)
            stats[at + 1 : at + 3, :] = jnp.zeros((2, size))
    else:
        stats[...] = stats_in[...]
    for i, (kv, shift) in enumerate(zip(blocks, shifts)):
        chips = distance(shift, cp)
        key_block = cp - 2 * chips
        for group, (q, g, st) in enumerate(((q_own, g_own, st_own), (q_sib, g_sib, st_sib))):
            row_block = cp if group == 0 else cp + 1 - 2 * lax.rem(cp, 2)

            def work(i=i, kv=kv, q=q, g=g, st=st, group=group, shift=shift, key_block=key_block, row_block=row_block):
                for head in range(2):
                    cols = pl.ds(head * HDIM, HDIM)
                    s = masked_scores(
                        kv[0], q[:, cols], st[...], row_block * size, key_block * size, shift == 0 and group == 0
                    )
                    dp = dot(kv[1], g[:, cols], NT)
                    if shift:
                        kept[2 * i][2 * group + head] = s
                        kept[2 * i + 1][2 * group + head] = dp
                    at = 3 * (2 * group + head)
                    m = stats[at : at + 1, :]
                    new = jnp.maximum(m, jnp.max(s, axis=0, keepdims=True))
                    p = jnp.exp2((s - new) * EXP_SCALE)
                    f = jnp.exp2((m - new) * EXP_SCALE)
                    stats[at : at + 1, :] = new
                    stats[at + 1 : at + 2, :] = stats[at + 1 : at + 2, :] * f + jnp.sum(p, axis=0, keepdims=True)
                    stats[at + 2 : at + 3, :] = stats[at + 2 : at + 3, :] * f + jnp.sum(p * dp, axis=0, keepdims=True)

            if shift == 0 and group == 0:
                work()
            elif shift == 0:
                pl.when(lax.rem(cp, 2) == 0)(work)
            else:
                pl.when(in_group >= 2 * chips)(work)


def merged(stats, other, at, other_at):
    m, m2 = stats[at : at + 1, :], other[other_at : other_at + 1, :]
    top = jnp.maximum(m, m2)
    f, f2 = jnp.exp2((m - top) * EXP_SCALE), jnp.exp2((m2 - top) * EXP_SCALE)
    total = stats[at + 1 : at + 2, :] * f + other[other_at + 1 : other_at + 2, :] * f2
    weighted = stats[at + 2 : at + 3, :] * f + other[other_at + 2 : other_at + 3, :] * f2
    return top * EXP_SCALE + jnp.log2(total), weighted / total


def grads_kernel(shift, first, pos_ref, *refs):
    if first:
        stats, other, kv, q_own, q_sib, g_own, g_sib, *refs = refs
        kept, (dq, dkv, fin, acc) = refs[:2], refs[2:]
        for s in range(4):
            log_sum, delta = merged(stats, other, 3 * s, 3 * (s ^ 2))
            fin[2 * s : 2 * s + 1, :] = log_sum
            fin[2 * s + 1 : 2 * s + 2, :] = delta
        dq[...] = jnp.zeros_like(dq)
    else:
        dq_in, fin, kv, q_own, q_sib, g_own, g_sib, *refs = refs
        kept, (dq, dkv, acc) = refs[:2], refs[2:]
        dq[...] = dq_in[...]
    cp = pos_ref[0]
    in_group = lax.rem(cp, GROUP)
    size = q_own.shape[0]
    acc[...] = jnp.zeros_like(acc)
    chips = distance(shift, cp)
    key_block = cp - 2 * chips
    k_t = kv[0].T
    for group, (q, g) in enumerate(((q_own, g_own), (q_sib, g_sib))):
        row_block = cp if group == 0 else cp + 1 - 2 * lax.rem(cp, 2)

        def work(q=q, g=g, group=group, row_block=row_block):
            for head in range(2):
                cols = pl.ds(head * HDIM, HDIM)
                if shift:
                    s = kept[0][2 * group + head]
                    dp = kept[1][2 * group + head]
                else:
                    s = masked_scores(kv[0], q[:, cols], kept[group][...], row_block * size, key_block * size, group == 0)
                    dp = dot(kv[1], g[:, cols], NT)
                at = 2 * (2 * group + head)
                p = jnp.exp2(s * EXP_SCALE - fin[at : at + 1, :])
                ds = (p * (dp - fin[at + 1 : at + 2, :])).astype(jnp.bfloat16)
                acc[0] += dot(ds, q[:, cols], NN)
                acc[1] += dot(p.astype(jnp.bfloat16), g[:, cols], NN)
                dq[group, cols, :] += dot(k_t, ds, NN)

        if shift == 0 and group == 0:
            work()
        elif shift == 0:
            pl.when(lax.rem(cp, 2) == 0)(work)
        else:
            pl.when(in_group >= 2 * chips)(work)
    dkv[...] = acc[...].astype(dkv.dtype)


def pack_kernel(keys, values, kv, sems):
    copies = [pltpu.make_async_copy(src, kv.at[i], sems.at[i]) for i, src in enumerate((keys, values))]
    for copy in copies:
        copy.start()
    for copy in copies:
        copy.wait()


def query_kernel(mine, other, out, done):
    done[...] = jnp.zeros_like(done)
    out[...] = ((mine[0] + other[...]) * SCALE).T.astype(out.dtype)


def add_kernel(total, part, out):
    out[...] = (total[...] + part[...].astype(jnp.float32)).astype(out.dtype)


def last_kernel(mine, other, _, grad_keys, grad_values):
    total = mine[...].astype(jnp.float32) + other[...].astype(jnp.float32)
    grad_keys[...] = (total[0] * SCALE).astype(grad_keys.dtype)
    grad_values[...] = total[1].astype(grad_values.dtype)


VM = pl.BlockSpec(memory_space=pltpu.VMEM)
SM = pl.BlockSpec(memory_space=pltpu.SMEM)


BLOCK_COST = pl.CostEstimate(flops=4 * 10 * 512 * 512 * 128, bytes_accessed=2**20, transcendentals=0)
LONG_COST = pl.CostEstimate(flops=40 * 10 * 512 * 512 * 128, bytes_accessed=2**20, transcendentals=0)
NO_COST = pl.CostEstimate(flops=0, bytes_accessed=2**10, transcendentals=0)


def simple(kernel, out, *args, cost=NO_COST):
    return pl.pallas_call(
        kernel,
        out_shape=out,
        in_specs=[VM] * len(args),
        out_specs=jax.tree.map(lambda _: VM, out),
        compiler_params=pltpu.CompilerParams(vmem_limit_bytes=8 * 2**20),
        cost_estimate=cost,
    )(*args)


def pack(keys, values):
    return pl.pallas_call(
        pack_kernel,
        out_shape=jax.ShapeDtypeStruct((2, *keys.shape), keys.dtype),
        in_specs=[pl.BlockSpec(memory_space=pltpu.HBM)] * 2,
        out_specs=VM,
        scratch_shapes=[pltpu.SemaphoreType.DMA((2,))],
        compiler_params=pltpu.CompilerParams(vmem_limit_bytes=8 * 2**20),
        cost_estimate=NO_COST,
        name="pack",
    )(keys, values)


def call_stats(shifts, cp, stats, blocks, rows):
    size = blocks[0].shape[1]
    remote = sum(shift > 0 for shift in shifts)
    kept = [jax.ShapeDtypeStruct((4, size, size), jnp.float32)] * (2 * remote)
    return pl.pallas_call(
        functools.partial(stats_kernel, shifts),
        out_shape=[jax.ShapeDtypeStruct((12, size), jnp.float32)] + kept,
        in_specs=[SM] + [VM] * (len(stats) + len(shifts) + len(rows)),
        out_specs=[VM] * (1 + len(kept)),
        compiler_params=pltpu.CompilerParams(vmem_limit_bytes=KERNEL_VMEM),
        cost_estimate=BLOCK_COST,
        name="stats",
    )(cp, *stats, *blocks, *rows)


def call_grads(shift, cp, before, block, rows, kept):
    size = block.shape[1]
    first = shift == 2
    out = [
        jax.ShapeDtypeStruct((2, 2 * HDIM, size), jnp.float32),
        jax.ShapeDtypeStruct((2, size, HDIM), jnp.float32 if shift == 0 else jnp.bfloat16),
    ]
    if first:
        out.append(jax.ShapeDtypeStruct((8, size), jnp.float32))
    return pl.pallas_call(
        functools.partial(grads_kernel, shift, first),
        out_shape=out,
        in_specs=[SM] + [VM] * (3 + 4 + 2),
        out_specs=[VM] * len(out),
        scratch_shapes=[pltpu.VMEM((2, size, HDIM), jnp.float32)],
        compiler_params=pltpu.CompilerParams(vmem_limit_bytes=KERNEL_VMEM),
        cost_estimate=NO_COST if shift == 0 else BLOCK_COST,
        name="grads",
    )(cp, *before, block, *rows[:4], *kept)


def body(query, keys, values, grad_out, doc_start):
    size = query.shape[0]
    position = lax.axis_index("cp").astype(jnp.int32)
    cp = position.reshape(1)
    kv = pack(keys, values)
    from1 = chip_shift(kv, 1, 1)
    from3 = chip_shift(kv, 3, 2)
    from2 = chip_shift(kv, 2, 3)
    starts = doc_start.reshape(1, size)
    rows = (query, core_swap(query), grad_out, core_swap(grad_out), starts, core_swap(starts))

    stats, *_ = call_stats((0,), cp, (), (kv,), rows)
    near = jax.ShapeDtypeStruct(keys.shape, keys.dtype)
    stats, s1, dp1 = call_stats((1,), cp, (stats,), (from1,), rows)
    stats, s2, dp2 = call_stats((2,), cp, (stats,), (from2,), rows)
    stats, s3, dp3 = call_stats((3,), cp, (stats,), (from3,), rows)

    dq, part2, fin = call_grads(2, cp, (stats, core_swap(stats)), from2, rows, (s2, dp2))
    back2 = chip_shift(part2, 2, 1)
    dq, part1 = call_grads(1, cp, (dq, fin), from1, rows, (s1, dp1))
    back1 = chip_shift(part1, 3, 3)
    dq, part3 = call_grads(3, cp, (dq, fin), from3, rows, (s3, dp3))
    back3 = chip_shift(part3, 1, 2)
    dq, own = call_grads(0, cp, (dq, fin), kv, rows, rows[4:])

    dq_other = core_swap(dq[1])
    token = jax.ShapeDtypeStruct((8, HDIM), jnp.float32)
    grad_query, done = simple(query_kernel, [jax.ShapeDtypeStruct(query.shape, query.dtype), token], dq, dq_other)
    total = jax.ShapeDtypeStruct(own.shape, own.dtype)
    half = simple(add_kernel, total, own, back2, cost=BLOCK_COST)
    half = simple(add_kernel, total, half, back1, cost=BLOCK_COST)
    half = simple(add_kernel, jax.ShapeDtypeStruct(kv.shape, kv.dtype), half, back3)
    other = hd_swap(half)
    grad_keys, grad_values = simple(last_kernel, [near] * 2, half, other, done)
    return grad_query, grad_keys, grad_values


def solution(mesh):
    in_specs = (P("cp", "hd"), P("cp", None), P("cp", None), P("cp", "hd"), P("cp"))
    out_specs = (P("cp", "hd"), P("cp", None), P("cp", None))
    return jax.shard_map(body, mesh=mesh, in_specs=in_specs, out_specs=out_specs, check_vma=False)
```

```python
import functools
import math

import jax
import jax.numpy as jnp
from jax import lax
from jax.experimental import pallas as pl
from jax.experimental.pallas import tpu as pltpu
from jax.sharding import PartitionSpec as P

HDIM = 128
GROUP = 8
SCALE = 1.0 / math.sqrt(HDIM)
EXP_SCALE = SCALE * math.log2(math.e)
MASKED = -1e30
FLOOR = -1e29
KERNEL_VMEM = 16 * 2**20

NT = (((1,), (1,)), ((), ()))
NN = (((1,), (0,)), ((), ()))
TN = (((0,), (0,)), ((), ()))


def dot(a, b, dims):
    return lax.dot_general(a, b, dims, preferred_element_type=jnp.float32)


def chip_shift(array, even, odd):
    n = lax.axis_size("cp")
    pairs = [(i, i - i % GROUP + (i % GROUP + 2 * (odd if i % 2 else even)) % GROUP) for i in range(n)]
    return lax.ppermute(array, "cp", pairs)


def core_swap(array):
    n = lax.axis_size("cp")
    return lax.ppermute(array, "cp", [(i, i ^ 1) for i in range(n)])


def hd_swap(array):
    return lax.ppermute(array, "hd", [(0, 1), (1, 0)])


def masked_scores(k, q, starts, row_base, key_base, diagonal):
    s = dot(k, q, NT)
    key_pos = key_base + lax.broadcasted_iota(jnp.int32, s.shape, 0)
    allowed = key_pos >= starts
    if diagonal:
        row_pos = row_base + lax.broadcasted_iota(jnp.int32, s.shape, 1)
        allowed = allowed & (key_pos <= row_pos)
    return jnp.where(allowed, s, MASKED)


def slot_distance(slot, cp):
    return slot if slot < 2 else slot + lax.rem(cp, 2) * (5 - 2 * slot)


def stats_kernel(slot, pos_ref, *refs):
    if slot:
        stats_in, *refs = refs
    if slot > 1:
        refs = refs[2:]
    kv, q_own, q_sib, g_own, g_sib, st_own, st_sib, stats, *kept = refs
    cp = pos_ref[0]
    in_group = lax.rem(cp, GROUP)
    size = q_own.shape[0]
    if slot:
        stats[...] = stats_in[...]
    else:
        for at in range(0, 12, 3):
            stats[at : at + 1, :] = jnp.full((1, size), FLOOR)
            stats[at + 1 : at + 3, :] = jnp.zeros((2, size))
    chips = slot_distance(slot, cp)
    key_block = cp - 2 * chips
    for group, (q, g, st) in enumerate(((q_own, g_own, st_own), (q_sib, g_sib, st_sib))):
        row_block = cp if group == 0 else cp + 1 - 2 * lax.rem(cp, 2)

        def work(q=q, g=g, st=st, group=group, row_block=row_block):
            for head in range(2):
                cols = pl.ds(head * HDIM, HDIM)
                s = masked_scores(kv[0], q[:, cols], st[...], row_block * size, key_block * size, slot == 0 and group == 0)
                dp = dot(kv[1], g[:, cols], NT)
                if slot:
                    kept[0][chips - 1, 2 * group + head] = s
                    kept[1][chips - 1, 2 * group + head] = dp
                at = 3 * (2 * group + head)
                m = stats[at : at + 1, :]
                new = jnp.maximum(m, jnp.max(s, axis=0, keepdims=True))
                p = jnp.exp2((s - new) * EXP_SCALE)
                f = jnp.exp2((m - new) * EXP_SCALE)
                stats[at : at + 1, :] = new
                stats[at + 1 : at + 2, :] = stats[at + 1 : at + 2, :] * f + jnp.sum(p, axis=0, keepdims=True)
                stats[at + 2 : at + 3, :] = stats[at + 2 : at + 3, :] * f + jnp.sum(p * dp, axis=0, keepdims=True)

        if slot == 0 and group == 0:
            work()
        elif slot == 0:
            pl.when(lax.rem(cp, 2) == 0)(work)
        else:
            pl.when(in_group >= 2 * chips)(work)


def merged(stats, other, at, other_at):
    m, m2 = stats[at : at + 1, :], other[other_at : other_at + 1, :]
    top = jnp.maximum(m, m2)
    f, f2 = jnp.exp2((m - top) * EXP_SCALE), jnp.exp2((m2 - top) * EXP_SCALE)
    total = stats[at + 1 : at + 2, :] * f + other[other_at + 1 : other_at + 2, :] * f2
    weighted = stats[at + 2 : at + 3, :] * f + other[other_at + 2 : other_at + 3, :] * f2
    return top * EXP_SCALE + jnp.log2(total), weighted / total


def stage_distance(stage, cp):
    odd = lax.rem(cp, 2)
    return (2, 3 - 2 * odd, 1 + 2 * odd, 0)[stage]


def grads_kernel(stage, pos_ref, *refs):
    before, (even, odd, q_own, q_sib, g_own, g_sib, kept0, kept1, dq, dkv, *refs) = refs[:2], refs[2:]
    acc = refs[-1]
    if stage == 0:
        (stats, other), fin = before, refs[0]
        for s in range(4):
            log_sum, delta = merged(stats, other, 3 * s, 3 * (s ^ 2))
            fin[2 * s : 2 * s + 1, :] = log_sum
            fin[2 * s + 1 : 2 * s + 2, :] = delta
        dq[...] = jnp.zeros_like(dq)
    else:
        dq_in, fin = before
        dq[...] = dq_in[...]
    cp = pos_ref[0]
    in_group = lax.rem(cp, GROUP)
    size = q_own.shape[0]
    acc[...] = jnp.zeros_like(acc)
    chips = stage_distance(stage, cp)
    k = even[0] if stage == 3 else jnp.where(lax.rem(cp, 2) == 0, even[0], odd[0])
    k_t = k.T
    for group, (q, g) in enumerate(((q_own, g_own), (q_sib, g_sib))):
        row_block = cp if group == 0 else cp + 1 - 2 * lax.rem(cp, 2)

        def work(q=q, g=g, group=group, row_block=row_block):
            for head in range(2):
                cols = pl.ds(head * HDIM, HDIM)
                if stage < 3:
                    s = kept0[chips - 1, 2 * group + head]
                    dp = kept1[chips - 1, 2 * group + head]
                else:
                    starts = (kept0, kept1)[group][...]
                    s = masked_scores(k, q[:, cols], starts, row_block * size, cp * size, group == 0)
                    dp = dot(even[1], g[:, cols], NT)
                at = 2 * (2 * group + head)
                p = jnp.exp2(s * EXP_SCALE - fin[at : at + 1, :])
                ds = (p * (dp - fin[at + 1 : at + 2, :])).astype(jnp.bfloat16)
                acc[0] += dot(ds, q[:, cols], NN)
                acc[1] += dot(p.astype(jnp.bfloat16), g[:, cols], NN)
                dq[group, cols, :] += dot(k_t, ds, NN)

        if stage == 3 and group == 0:
            work()
        elif stage == 3:
            pl.when(lax.rem(cp, 2) == 0)(work)
        else:
            pl.when(in_group >= 2 * chips)(work)
    dkv[...] = acc[...].astype(dkv.dtype)


def query_kernel(mine, other, out, done):
    done[...] = jnp.zeros_like(done)
    out[...] = ((mine[0] + other[...]) * SCALE).T.astype(out.dtype)


def add_kernel(total, part, out):
    out[...] = (total[...] + part[...].astype(jnp.float32)).astype(out.dtype)


def last_kernel(mine, other, _, grad_keys, grad_values):
    total = mine[...].astype(jnp.float32) + other[...].astype(jnp.float32)
    grad_keys[...] = (total[0] * SCALE).astype(grad_keys.dtype)
    grad_values[...] = total[1].astype(grad_values.dtype)


VM = pl.BlockSpec(memory_space=pltpu.VMEM)
SM = pl.BlockSpec(memory_space=pltpu.SMEM)


BLOCK_COST = pl.CostEstimate(flops=10 * 512 * 512 * 128 // 10, bytes_accessed=2**10, transcendentals=0)
LONG_COST = pl.CostEstimate(flops=40 * 10 * 512 * 512 * 128, bytes_accessed=2**20, transcendentals=0)
NO_COST = pl.CostEstimate(flops=0, bytes_accessed=2**10, transcendentals=0)


def simple(kernel, out, *args, cost=NO_COST):
    return pl.pallas_call(
        kernel,
        out_shape=out,
        in_specs=[VM] * len(args),
        out_specs=jax.tree.map(lambda _: VM, out),
        compiler_params=pltpu.CompilerParams(vmem_limit_bytes=8 * 2**20),
        cost_estimate=cost,
    )(*args)


def call_stats(slot, cp, before, kv, rows):
    size = kv.shape[1]
    out = [jax.ShapeDtypeStruct((12, size), jnp.float32)]
    if slot:
        out += [jax.ShapeDtypeStruct((3, 4, size, size), jnp.float32)] * 2
    kept = len(before[1:])
    return pl.pallas_call(
        functools.partial(stats_kernel, slot),
        out_shape=out,
        in_specs=[SM] + [VM] * len(before[:1]) + [pl.BlockSpec(memory_space=pl.ANY)] * kept + [VM] * (1 + len(rows)),
        out_specs=[VM] * len(out),
        input_output_aliases={2: 1, 3: 2} if kept else {},
        compiler_params=pltpu.CompilerParams(vmem_limit_bytes=KERNEL_VMEM),
        cost_estimate=BLOCK_COST,
        name="stats",
    )(cp, *before, kv, *rows)


def call_grads(stage, cp, before, even, odd, rows, kept):
    size = even.shape[1]
    out = [
        jax.ShapeDtypeStruct((2, 2 * HDIM, size), jnp.float32),
        jax.ShapeDtypeStruct((2, size, HDIM), jnp.float32 if stage == 3 else jnp.bfloat16),
    ]
    if stage == 0:
        out.append(jax.ShapeDtypeStruct((8, size), jnp.float32))
    return pl.pallas_call(
        functools.partial(grads_kernel, stage),
        out_shape=out,
        in_specs=[SM] + [VM] * 10,
        out_specs=[VM] * len(out),
        scratch_shapes=[pltpu.VMEM((2, size, HDIM), jnp.float32)],
        compiler_params=pltpu.CompilerParams(vmem_limit_bytes=KERNEL_VMEM),
        cost_estimate=NO_COST if stage == 3 else BLOCK_COST,
        name="grads",
    )(cp, *before, even, odd, *rows[:4], *kept)


def body(query, keys, values, grad_out, doc_start):
    size = query.shape[0]
    position = lax.axis_index("cp").astype(jnp.int32)
    cp = position.reshape(1)
    kv = jnp.where(lax.broadcasted_iota(jnp.int32, (2, *keys.shape), 0) == 0, keys[None], values[None])
    slot1 = chip_shift(kv, 1, 1)
    slot2 = chip_shift(kv, 2, 3)
    slot3 = chip_shift(kv, 3, 2)
    starts = doc_start.reshape(1, size)
    rows = (query, core_swap(query), grad_out, core_swap(grad_out), starts, core_swap(starts))

    (stats,) = call_stats(0, cp, (), kv, rows)
    before = call_stats(1, cp, (stats,), slot1, rows)
    before = call_stats(2, cp, before, slot2, rows)
    stats, *kept = call_stats(3, cp, before, slot3, rows)

    dq, part, fin = call_grads(0, cp, (stats, core_swap(stats)), slot2, slot3, rows, kept)
    back_a = chip_shift(part, 2, 2)
    dq, part = call_grads(1, cp, (dq, fin), slot3, slot1, rows, kept)
    back_b = chip_shift(part, 1, 3)
    dq, part = call_grads(2, cp, (dq, fin), slot1, slot2, rows, kept)
    back_c = chip_shift(part, 3, 1)
    dq, own = call_grads(3, cp, (dq, fin), kv, kv, rows, rows[4:])

    dq_other = core_swap(dq[1])
    token = jax.ShapeDtypeStruct((8, HDIM), jnp.float32)
    grad_query, done = simple(query_kernel, [jax.ShapeDtypeStruct(query.shape, query.dtype), token], dq, dq_other)
    total = jax.ShapeDtypeStruct(own.shape, own.dtype)
    half = simple(add_kernel, total, own, back_a, cost=BLOCK_COST)
    half = simple(add_kernel, total, half, back_b, cost=LONG_COST)
    half = simple(add_kernel, jax.ShapeDtypeStruct(kv.shape, kv.dtype), half, back_c)
    other = hd_swap(half)
    near = jax.ShapeDtypeStruct(keys.shape, keys.dtype)
    grad_keys, grad_values = simple(last_kernel, [near] * 2, half, other, done)
    return grad_query, grad_keys, grad_values


def solution(mesh):
    in_specs = (P("cp", "hd"), P("cp", None), P("cp", None), P("cp", "hd"), P("cp"))
    out_specs = (P("cp", "hd"), P("cp", None), P("cp", None))
    return jax.shard_map(body, mesh=mesh, in_specs=in_specs, out_specs=out_specs, check_vma=False)
```

```python
import functools
import math

import jax
import jax.numpy as jnp
from jax import lax
from jax.experimental import pallas as pl
from jax.experimental.pallas import tpu as pltpu
from jax.sharding import PartitionSpec as P

HDIM = 128
GROUP = 8
SCALE = 1.0 / math.sqrt(HDIM)
EXP_SCALE = SCALE * math.log2(math.e)
MASKED = -1e30
FLOOR = -1e29
KERNEL_VMEM = 16 * 2**20

NT = (((1,), (1,)), ((), ()))
NN = (((1,), (0,)), ((), ()))
TN = (((0,), (0,)), ((), ()))


def dot(a, b, dims):
    return lax.dot_general(a, b, dims, preferred_element_type=jnp.float32)


def chip_shift(array, even, odd):
    n = lax.axis_size("cp")
    pairs = [(i, i - i % GROUP + (i % GROUP + 2 * (odd if i % 2 else even)) % GROUP) for i in range(n)]
    return lax.ppermute(array, "cp", pairs)


def chip_permute(array, even, odd):
    n = lax.axis_size("cp")
    pairs = [(i, i - i % GROUP + 2 * (odd if i % 2 else even)[i % GROUP // 2] + i % 2) for i in range(n)]
    return lax.ppermute(array, "cp", pairs)


def core_swap(array):
    n = lax.axis_size("cp")
    return lax.ppermute(array, "cp", [(i, i ^ 1) for i in range(n)])


def hd_swap(array):
    return lax.ppermute(array, "hd", [(0, 1), (1, 0)])


def masked_scores(k, q, starts, row_base, key_base, diagonal):
    s = dot(k, q, NT)
    key_pos = key_base + lax.broadcasted_iota(jnp.int32, s.shape, 0)
    allowed = key_pos >= starts
    if diagonal:
        row_pos = row_base + lax.broadcasted_iota(jnp.int32, s.shape, 1)
        allowed = allowed & (key_pos <= row_pos)
    return jnp.where(allowed, s, MASKED)


def slot_distance(slot, cp):
    return slot if slot < 2 else slot + lax.rem(cp, 2) * (5 - 2 * slot)


def stats_kernel(slot, pos_ref, *refs):
    if slot == 0:
        kv, q_own, g_own, st_own, stats, *copies = refs
        for src, dst in zip((q_own, g_own, st_own), copies):
            dst[...] = src[...]
        rows = ((q_own, g_own, st_own),)
    else:
        stats_in, *refs = refs
        if slot == 1:
            own, *refs = refs
        else:
            refs = refs[2:]
        kv, q_own, q_sib, g_own, g_sib, st_own, st_sib, stats, *kept = refs
        rows = ((q_own, g_own, st_own), (q_sib, g_sib, st_sib))
    cp = pos_ref[0]
    in_group = lax.rem(cp, GROUP)
    size = kv.shape[1]
    if slot:
        stats[...] = stats_in[...]
    else:
        for at in range(0, 12, 3):
            stats[at : at + 1, :] = jnp.full((1, size), FLOOR)
            stats[at + 1 : at + 3, :] = jnp.zeros((2, size))
    chips = slot_distance(slot, cp)

    def work(kv, group, chips, keep):
        q, g, st = rows[group]
        key_base = (cp - 2 * chips) * size
        row_base = (cp if group == 0 else cp + 1 - 2 * lax.rem(cp, 2)) * size
        for head in range(2):
            cols = pl.ds(head * HDIM, HDIM)
            s = masked_scores(kv[0], q[:, cols], st[...], row_base, key_base, slot == 0)
            dp = dot(kv[1], g[:, cols], NT)
            if keep:
                kept[0][chips - 1, 2 * group + head] = s
                kept[1][chips - 1, 2 * group + head] = dp
            at = 3 * (2 * group + head)
            m = stats[at : at + 1, :]
            new = jnp.maximum(m, jnp.max(s, axis=0, keepdims=True))
            p = jnp.exp2((s - new) * EXP_SCALE)
            f = jnp.exp2((m - new) * EXP_SCALE)
            stats[at : at + 1, :] = new
            stats[at + 1 : at + 2, :] = stats[at + 1 : at + 2, :] * f + jnp.sum(p, axis=0, keepdims=True)
            stats[at + 2 : at + 3, :] = stats[at + 2 : at + 3, :] * f + jnp.sum(p * dp, axis=0, keepdims=True)

    if slot == 0:
        work(kv, 0, 0, False)
    if slot == 1:
        pl.when(lax.rem(cp, 2) == 0)(lambda: work(own, 1, 0, False))
    if slot:

        @pl.when(in_group >= 2 * chips)
        def _():
            work(kv, 0, chips, True)
            work(kv, 1, chips, True)


def merged(stats, other, at, other_at):
    m, m2 = stats[at : at + 1, :], other[other_at : other_at + 1, :]
    top = jnp.maximum(m, m2)
    f, f2 = jnp.exp2((m - top) * EXP_SCALE), jnp.exp2((m2 - top) * EXP_SCALE)
    total = stats[at + 1 : at + 2, :] * f + other[other_at + 1 : other_at + 2, :] * f2
    weighted = stats[at + 2 : at + 3, :] * f + other[other_at + 2 : other_at + 3, :] * f2
    return top * EXP_SCALE + jnp.log2(total), weighted / total


def stage_distance(stage, cp):
    odd = lax.rem(cp, 2)
    return (2, 3 - 2 * odd, 1 + 2 * odd, 0)[stage]


def grads_kernel(stage, pos_ref, *refs):
    before, (even, odd, q_own, q_sib, g_own, g_sib, kept0, kept1, dq, dkv, *refs) = refs[:2], refs[2:]
    acc = refs[-1]
    if stage == 0:
        (stats, other), fin = before, refs[0]
        for s in range(4):
            log_sum, delta = merged(stats, other, 3 * s, 3 * (s ^ 2))
            fin[2 * s : 2 * s + 1, :] = log_sum
            fin[2 * s + 1 : 2 * s + 2, :] = delta
        dq[...] = jnp.zeros_like(dq)
    else:
        dq_in, fin = before
        dq[...] = dq_in[...]
    cp = pos_ref[0]
    in_group = lax.rem(cp, GROUP)
    size = q_own.shape[0]
    acc[...] = jnp.zeros_like(acc)
    chips = stage_distance(stage, cp)
    k = even[0] if stage == 3 else jnp.where(lax.rem(cp, 2) == 0, even[0], odd[0])
    k_t = k.T
    for group, (q, g) in enumerate(((q_own, g_own), (q_sib, g_sib))):
        row_block = cp if group == 0 else cp + 1 - 2 * lax.rem(cp, 2)

        def work(q=q, g=g, group=group, row_block=row_block):
            for head in range(2):
                cols = pl.ds(head * HDIM, HDIM)
                if stage < 3:
                    s = kept0[chips - 1, 2 * group + head]
                    dp = kept1[chips - 1, 2 * group + head]
                else:
                    starts = (kept0, kept1)[group][...]
                    s = masked_scores(k, q[:, cols], starts, row_block * size, cp * size, group == 0)
                    dp = dot(even[1], g[:, cols], NT)
                at = 2 * (2 * group + head)
                p = jnp.exp2(s * EXP_SCALE - fin[at : at + 1, :])
                ds = (p * (dp - fin[at + 1 : at + 2, :])).astype(jnp.bfloat16)
                acc[0] += dot(ds, q[:, cols], NN)
                acc[1] += dot(p.astype(jnp.bfloat16), g[:, cols], NN)
                dq[group, cols, :] += dot(k_t, ds, NN)

        if stage == 3 and group == 0:
            work()
        elif stage == 3:
            pl.when(lax.rem(cp, 2) == 0)(work)
        else:
            pl.when(in_group >= 2 * chips)(work)
    dkv[...] = acc[...].astype(dkv.dtype)


def query_kernel(mine, other, out, done):
    done[...] = jnp.zeros_like(done)
    out[...] = ((mine[0] + other[...]) * SCALE).T.astype(out.dtype)


def add_kernel(total, part, out):
    out[...] = (total[...] + part[...].astype(jnp.float32)).astype(out.dtype)


def last_kernel(mine, other, _, grad_keys, grad_values):
    total = mine[...].astype(jnp.float32) + other[...].astype(jnp.float32)
    grad_keys[...] = (total[0] * SCALE).astype(grad_keys.dtype)
    grad_values[...] = total[1].astype(grad_values.dtype)


VM = pl.BlockSpec(memory_space=pltpu.VMEM)
SM = pl.BlockSpec(memory_space=pltpu.SMEM)


BLOCK_COST = pl.CostEstimate(flops=10 * 512 * 512 * 128 // 10, bytes_accessed=2**10, transcendentals=0)
LONG_COST = pl.CostEstimate(flops=40 * 10 * 512 * 512 * 128, bytes_accessed=2**20, transcendentals=0)
NO_COST = pl.CostEstimate(flops=0, bytes_accessed=2**10, transcendentals=0)


def simple(kernel, out, *args, cost=NO_COST):
    return pl.pallas_call(
        kernel,
        out_shape=out,
        in_specs=[VM] * len(args),
        out_specs=jax.tree.map(lambda _: VM, out),
        compiler_params=pltpu.CompilerParams(vmem_limit_bytes=8 * 2**20),
        cost_estimate=cost,
    )(*args)


def call_stats(slot, cp, before, kv, rows):
    size = kv.shape[1]
    out = [jax.ShapeDtypeStruct((12, size), jnp.float32)]
    if slot:
        out += [jax.ShapeDtypeStruct((3, 4, size, size), jnp.float32)] * 2
    else:
        out += [jax.ShapeDtypeStruct(a.shape, a.dtype) for a in rows]
    in_specs = [SM] + [VM] * (len(before) + 1 + len(rows))
    if slot > 1:
        in_specs[2:4] = [pl.BlockSpec(memory_space=pl.ANY)] * 2
    return pl.pallas_call(
        functools.partial(stats_kernel, slot),
        out_shape=out,
        in_specs=in_specs,
        out_specs=[VM] * len(out),
        input_output_aliases={2: 1, 3: 2} if slot > 1 else {},
        compiler_params=pltpu.CompilerParams(vmem_limit_bytes=KERNEL_VMEM),
        cost_estimate=NO_COST,
        name="stats",
    )(cp, *before, kv, *rows)


def call_grads(stage, cp, before, even, odd, rows, kept):
    size = even.shape[1]
    out = [
        jax.ShapeDtypeStruct((2, 2 * HDIM, size), jnp.float32),
        jax.ShapeDtypeStruct((2, size, HDIM), jnp.float32 if stage == 3 else jnp.bfloat16),
    ]
    if stage == 0:
        out.append(jax.ShapeDtypeStruct((8, size), jnp.float32))
    return pl.pallas_call(
        functools.partial(grads_kernel, stage),
        out_shape=out,
        in_specs=[SM] + [VM] * 10,
        out_specs=[VM] * len(out),
        scratch_shapes=[pltpu.VMEM((2, size, HDIM), jnp.float32)],
        compiler_params=pltpu.CompilerParams(vmem_limit_bytes=KERNEL_VMEM),
        cost_estimate=NO_COST if stage == 3 else BLOCK_COST,
        name="grads",
    )(cp, *before, even, odd, *rows[:4], *kept)


def body(query, keys, values, grad_out, doc_start):
    size = query.shape[0]
    position = lax.axis_index("cp").astype(jnp.int32)
    cp = position.reshape(1)
    kv = jnp.where(lax.broadcasted_iota(jnp.int32, (2, *keys.shape), 0) == 0, keys[None], values[None])
    slot1 = chip_shift(kv, 1, 1)
    slot2 = chip_shift(kv, 2, 3)
    slot3 = chip_shift(kv, 3, 2)
    starts = doc_start.reshape(1, size)
    kv, near_query, near_grad = lax.optimization_barrier((kv, query, grad_out))
    far_query, near_starts = lax.optimization_barrier((core_swap(near_query), starts))
    far_grad, far_starts = core_swap(near_grad), core_swap(near_starts)

    stats, *own_rows = call_stats(0, cp, (), kv, (query, grad_out, starts))
    rows = (own_rows[0], far_query, own_rows[1], far_grad, own_rows[2], far_starts)
    before = call_stats(1, cp, (stats, kv), slot1, rows)
    before = call_stats(2, cp, before, slot2, rows)
    stats, *kept = call_stats(3, cp, before, slot3, rows)

    dq, part, fin = call_grads(0, cp, (stats, core_swap(stats)), slot2, slot3, rows, kept)
    back_a = chip_permute(part, (3, 2, 0, 1), (3, 2, 0, 1))
    dq, part = call_grads(1, cp, (dq, fin), slot3, slot1, rows, kept)
    back_b = chip_shift(part, 1, 3)
    dq, part = call_grads(2, cp, (dq, fin), slot1, slot2, rows, kept)
    back_c = chip_shift(part, 3, 1)
    dq, own = call_grads(3, cp, (dq, fin), kv, kv, rows, rows[4:])

    dq_other = core_swap(dq[1])
    token = jax.ShapeDtypeStruct((8, HDIM), jnp.float32)
    grad_query, done = simple(query_kernel, [jax.ShapeDtypeStruct(query.shape, query.dtype), token], dq, dq_other)
    total = jax.ShapeDtypeStruct(own.shape, own.dtype)
    half = simple(add_kernel, total, own, back_a, cost=BLOCK_COST)
    half = simple(add_kernel, total, half, back_b, cost=LONG_COST)
    half = simple(add_kernel, jax.ShapeDtypeStruct(kv.shape, kv.dtype), half, back_c)
    other = hd_swap(half)
    near = jax.ShapeDtypeStruct(keys.shape, keys.dtype)
    grad_keys, grad_values = simple(last_kernel, [near] * 2, half, other, done)
    return grad_query, grad_keys, grad_values


def solution(mesh):
    in_specs = (P("cp", "hd"), P("cp", None), P("cp", None), P("cp", "hd"), P("cp"))
    out_specs = (P("cp", "hd"), P("cp", None), P("cp", None))
    return jax.shard_map(body, mesh=mesh, in_specs=in_specs, out_specs=out_specs, check_vma=False)
```

```python
import functools
import math

import jax
import jax.numpy as jnp
from jax import lax
from jax.experimental import pallas as pl
from jax.experimental.pallas import tpu as pltpu
from jax.sharding import PartitionSpec as P

HDIM = 128
GROUP = 8
SCALE = 1.0 / math.sqrt(HDIM)
EXP_SCALE = SCALE * math.log2(math.e)
MASKED = -1e30
FLOOR = -1e29
KERNEL_VMEM = 16 * 2**20
KEYS = 512

NT = (((1,), (1,)), ((), ()))
NN = (((1,), (0,)), ((), ()))
TN = (((0,), (0,)), ((), ()))


def dot(a, b, dims):
    return lax.dot_general(a, b, dims, preferred_element_type=jnp.float32)


def chip_shift(array, even, odd):
    n = lax.axis_size("cp")
    pairs = [(i, i - i % GROUP + (i % GROUP + 2 * (odd if i % 2 else even)) % GROUP) for i in range(n)]
    return lax.ppermute(array, "cp", pairs)


def chip_permute(array, even, odd):
    n = lax.axis_size("cp")
    to = [(odd if i % 2 else even)[i % GROUP // 2] for i in range(n)]
    pairs = [(i, i - i % GROUP + 2 * to[i] + i % 2) for i in range(n) if to[i] is not None]
    return lax.ppermute(array, "cp", pairs)


def core_swap(array):
    n = lax.axis_size("cp")
    return lax.ppermute(array, "cp", [(i, i ^ 1) for i in range(n)])


def hd_swap(array):
    return lax.ppermute(array, "hd", [(0, 1), (1, 0)])


def masked_scores(k, q, starts, row_base, key_base, diagonal):
    s = dot(k, q, NT)
    key_pos = key_base + lax.broadcasted_iota(jnp.int32, s.shape, 0)
    allowed = key_pos >= starts
    if diagonal:
        row_pos = row_base + lax.broadcasted_iota(jnp.int32, s.shape, 1)
        allowed = allowed & (key_pos <= row_pos)
    return jnp.where(allowed, s, MASKED)


def slot_distance(slot, cp):
    return slot if slot < 2 else slot + lax.rem(cp, 2) * (5 - 2 * slot)


def stats_kernel(step, slot, groups, pos_ref, *refs):
    if step == 0:
        kv, q_own, g_own, st_own, stats, *copies = refs
        for src, dst in zip((q_own, g_own, st_own), copies):
            dst[...] = src[...]
        rows = ((q_own, g_own, st_own),)
    else:
        stats_in, *refs = refs
        if step == 1:
            own, *refs = refs
        else:
            refs = refs[2:]
        kv, q_own, q_sib, g_own, g_sib, st_own, st_sib, stats, *kept = refs
        rows = ((q_own, g_own, st_own), (q_sib, g_sib, st_sib))
    cp = pos_ref[0]
    in_group = lax.rem(cp, GROUP)
    size = kv.shape[1]
    base = 6 * groups[0]
    if step:
        stats[...] = stats_in[base : base + stats.shape[0], :]
    else:
        for at in range(0, 12, 3):
            stats[at : at + 1, :] = jnp.full((1, size), FLOOR)
            stats[at + 1 : at + 3, :] = jnp.zeros((2, size))
    chips = slot_distance(slot, cp)

    def work(kv, group, chips, keep):
        q, g, st = rows[group]
        key_base = (cp - 2 * chips) * size
        row_base = (cp if group == 0 else cp + 1 - 2 * lax.rem(cp, 2)) * size
        for head in range(2):
            cols = pl.ds(head * HDIM, HDIM)
            at = 3 * (2 * group + head) - base
            for first in range(0, size, KEYS):
                keys = pl.ds(first, KEYS)
                s = masked_scores(kv[0, keys], q[:, cols], st[...], row_base, key_base + first, step == 0)
                dp = dot(kv[1, keys], g[:, cols], NT)
                if keep:
                    kept[0][chips - 1, 2 * group + head, keys] = s
                    kept[1][chips - 1, 2 * group + head, keys] = dp
                m = stats[at : at + 1, :]
                new = jnp.maximum(m, jnp.max(s, axis=0, keepdims=True))
                p = jnp.exp2((s - new) * EXP_SCALE)
                f = jnp.exp2((m - new) * EXP_SCALE)
                stats[at : at + 1, :] = new
                stats[at + 1 : at + 2, :] = stats[at + 1 : at + 2, :] * f + jnp.sum(p, axis=0, keepdims=True)
                stats[at + 2 : at + 3, :] = stats[at + 2 : at + 3, :] * f + jnp.sum(p * dp, axis=0, keepdims=True)

    if step == 0:
        work(kv, 0, 0, False)
    if step == 1:
        pl.when(lax.rem(cp, 2) == 0)(lambda: work(own, 1, 0, False))
    if step:

        @pl.when(in_group >= 2 * chips)
        def _():
            for group in groups:
                work(kv, group, chips, True)


def merged(stats, other, at):
    m, m2 = stats[at : at + 1, :], other[at : at + 1, :]
    top = jnp.maximum(m, m2)
    f, f2 = jnp.exp2((m - top) * EXP_SCALE), jnp.exp2((m2 - top) * EXP_SCALE)
    total = stats[at + 1 : at + 2, :] * f + other[at + 1 : at + 2, :] * f2
    weighted = stats[at + 2 : at + 3, :] * f + other[at + 2 : at + 3, :] * f2
    return top * EXP_SCALE + jnp.log2(total), weighted / total


def stage_distance(stage, cp):
    odd = lax.rem(cp, 2)
    return (2, 1 + 2 * odd, 3 - 2 * odd, 0)[stage]


def add_grads(q, g, s, dp, fin, at, acc, cols):
    p = jnp.exp2(s * EXP_SCALE - fin[at : at + 1, :])
    ds = (p * (dp - fin[at + 1 : at + 2, :])).astype(jnp.bfloat16)
    acc[0] += dot(ds, q[:, cols], NN)
    acc[1] += dot(p.astype(jnp.bfloat16), g[:, cols], NN)
    return ds


def first_kernel(group, pos_ref, *refs):
    if group == 0:
        acc_in, *refs = refs
    stats, other, q, g, kept0, kept1, kept, fin, *refs = refs
    acc = refs[-1]
    for head in range(2):
        log_sum, delta = merged(stats, other, 3 * head)
        fin[2 * head : 2 * head + 1, :] = log_sum
        fin[2 * head + 1 : 2 * head + 2, :] = delta
    acc[...] = acc_in[...] if group == 0 else jnp.zeros_like(acc)
    cp = pos_ref[0]
    chips = stage_distance(0, cp)

    @pl.when(lax.rem(cp, GROUP) >= 2 * chips)
    def _():
        for head in range(2):
            at = 2 * group + head
            cols = pl.ds(head * HDIM, HDIM)
            kept[head] = add_grads(q, g, kept0[chips - 1, at], kept1[chips - 1, at], fin, 2 * head, acc, cols)

    if group == 0:
        refs[0][...] = acc[...].astype(jnp.bfloat16)


def grads_kernel(stage, pos_ref, *refs):
    if stage > 1:
        dq_in, refs = refs[:2], refs[2:]
    (fin_own, fin_sib), refs = refs[:2], refs[2:]
    even, odd, q_own, q_sib, g_own, g_sib, kept0, kept1, *refs = refs
    if stage == 3:
        first_even, first_odd, *first, dq_own, dq_sib, dkv, acc = refs
    else:
        dq_own, dq_sib, dkv, acc = refs
    cp = pos_ref[0]
    in_group = lax.rem(cp, GROUP)
    even_core = lax.rem(cp, 2) == 0
    size = q_own.shape[0]
    acc[...] = jnp.zeros_like(acc)
    for i, dq in enumerate((dq_own, dq_sib)):
        dq[...] = dq_in[i][...] if stage > 1 else jnp.zeros_like(dq)
    chips = stage_distance(stage, cp)
    k = even[0] if stage == 3 else jnp.where(even_core, even[0], odd[0])
    k_t = k.T
    groups = ((q_own, g_own, fin_own, dq_own), (q_sib, g_sib, fin_sib, dq_sib))
    for group, (q, g, fin, dq) in enumerate(groups):

        def work(group=group, q=q, g=g, fin=fin, dq=dq):
            for head in range(2):
                cols = pl.ds(head * HDIM, HDIM)
                if stage < 3:
                    s = kept0[chips - 1, 2 * group + head]
                    dp = kept1[chips - 1, 2 * group + head]
                else:
                    starts = (kept0, kept1)[group][...]
                    s = masked_scores(k, q[:, cols], starts, (cp + group) * size, cp * size, group == 0)
                    dp = dot(even[1], g[:, cols], NT)
                ds = add_grads(q, g, s, dp, fin, 2 * head, acc, cols)
                dq[cols, :] += dot(k_t, ds, NN)

        if stage == 3 and group == 0:
            work()
        elif stage == 3:
            pl.when(even_core)(work)
        else:
            pl.when(in_group >= 2 * chips)(work)
    dkv[...] = acc[...].astype(dkv.dtype)
    if stage == 3:

        @pl.when(in_group >= 2 * stage_distance(0, cp))
        def _():
            first_t = jnp.where(even_core, first_even[0], first_odd[0]).T
            for ds, dq in zip(first, (dq_own, dq_sib)):
                for head in range(2):
                    dq[pl.ds(head * HDIM, HDIM), :] += dot(first_t, ds[head], NN)


def query_kernel(mine, other, out, done):
    done[...] = jnp.zeros_like(done)
    out[...] = ((mine[...] + other[...]) * SCALE).T.astype(out.dtype)


def add_kernel(total, part, out):
    out[...] = (total[...] + part[...].astype(jnp.float32)).astype(out.dtype)


def last_kernel(mine, other, _, grad_keys, grad_values):
    total = mine[...].astype(jnp.float32) + other[...].astype(jnp.float32)
    grad_keys[...] = (total[0] * SCALE).astype(grad_keys.dtype)
    grad_values[...] = total[1].astype(grad_values.dtype)


VM = pl.BlockSpec(memory_space=pltpu.VMEM)
SM = pl.BlockSpec(memory_space=pltpu.SMEM)


BLOCK_COST = pl.CostEstimate(flops=10 * 512 * 512 * 128 // 10, bytes_accessed=2**10, transcendentals=0)
LONG_COST = pl.CostEstimate(flops=40 * 10 * 512 * 512 * 128, bytes_accessed=2**20, transcendentals=0)
NO_COST = pl.CostEstimate(flops=0, bytes_accessed=2**10, transcendentals=0)


def simple(kernel, out, *args, cost=NO_COST):
    return pl.pallas_call(
        kernel,
        out_shape=out,
        in_specs=[VM] * len(args),
        out_specs=jax.tree.map(lambda _: VM, out),
        compiler_params=pltpu.CompilerParams(vmem_limit_bytes=8 * 2**20),
        cost_estimate=cost,
    )(*args)


def call_stats(step, slot, cp, before, kv, rows, groups=(0, 1)):
    size = kv.shape[1]
    out = [jax.ShapeDtypeStruct((6 * len(groups), size), jnp.float32)]
    if step:
        out += [jax.ShapeDtypeStruct((3, 4, size, size), jnp.float32)] * 2
    else:
        out += [jax.ShapeDtypeStruct(a.shape, a.dtype) for a in rows]
    in_specs = [SM] + [VM] * (len(before) + 1 + len(rows))
    if step > 1:
        in_specs[2:4] = [pl.BlockSpec(memory_space=pl.ANY)] * 2
    return pl.pallas_call(
        functools.partial(stats_kernel, step, slot, groups),
        out_shape=out,
        in_specs=in_specs,
        out_specs=[VM] * len(out),
        input_output_aliases={2: 1, 3: 2} if step > 1 else {},
        compiler_params=pltpu.CompilerParams(vmem_limit_bytes=KERNEL_VMEM),
        cost_estimate=NO_COST,
        name="stats",
    )(cp, *before, kv, *rows)


def call_grads(kernel, cp, out, args, cost, scratch=()):
    return pl.pallas_call(
        kernel,
        out_shape=out,
        in_specs=[SM] + [VM] * len(args),
        out_specs=[VM] * len(out),
        scratch_shapes=scratch,
        compiler_params=pltpu.CompilerParams(vmem_limit_bytes=KERNEL_VMEM),
        cost_estimate=cost,
        name="grads",
    )(cp, *args)


def call_first(group, cp, before, rows, kept):
    size = rows[0].shape[0]
    total = (2, size, HDIM)
    out = [jax.ShapeDtypeStruct((2, size, size), jnp.bfloat16), jax.ShapeDtypeStruct((4, size), jnp.float32)]
    out.append(jax.ShapeDtypeStruct(total, jnp.float32 if group else jnp.bfloat16))
    scratch = [] if group else [pltpu.VMEM(total, jnp.float32)]
    args = (*before, rows[group], rows[2 + group], *kept)
    return call_grads(functools.partial(first_kernel, group), cp, out, args, NO_COST if group else BLOCK_COST, scratch)


def call_stage(stage, cp, dq, fin, blocks, rows, kept):
    size = rows[0].shape[0]
    total = (2, size, HDIM)
    out = [jax.ShapeDtypeStruct((2 * HDIM, size), jnp.float32)] * 2
    out.append(jax.ShapeDtypeStruct(total, jnp.float32 if stage == 3 else jnp.bfloat16))
    args = (*dq, *fin, *blocks, *rows[:4], *kept)
    cost = NO_COST if stage == 3 else BLOCK_COST
    *dq, part = call_grads(functools.partial(grads_kernel, stage), cp, out, args, cost, [pltpu.VMEM(total, jnp.float32)])
    return dq, part


def body(query, keys, values, grad_out, doc_start):
    size = query.shape[0]
    position = lax.axis_index("cp").astype(jnp.int32)
    cp = position.reshape(1)
    kv = jnp.where(lax.broadcasted_iota(jnp.int32, (2, *keys.shape), 0) == 0, keys[None], values[None])
    slot1 = chip_shift(kv, 1, 1)
    slot2 = chip_permute(kv, (2, 3, 0, 1), (3, 0, 1, 2))
    slot3 = chip_permute(kv, (3, 0, 1, 2), (2, 3, 0, 1))
    starts = doc_start.reshape(1, size)
    kv, near_query, near_grad = lax.optimization_barrier((kv, query, grad_out))
    far_query, near_starts = lax.optimization_barrier((core_swap(near_query), starts))
    far_grad, far_starts = core_swap(near_grad), core_swap(near_starts)

    stats, *own_rows = call_stats(0, 0, cp, (), kv, (query, grad_out, starts))
    rows = (own_rows[0], far_query, own_rows[1], far_grad, own_rows[2], far_starts)
    before = call_stats(1, 1, cp, (stats, kv), slot1, rows)
    before = call_stats(2, 2, cp, before, slot2, rows)
    stats = before[0]
    near, *kept = call_stats(3, 3, cp, before, slot3, rows, (0,))
    far_other = core_swap(near)
    far, *kept = call_stats(3, 3, cp, (stats, *kept), slot3, rows, (1,))
    near_other = core_swap(far)

    ds_far, fin_far, part = call_first(1, cp, (far, far_other), rows, kept)
    ds_near, fin_near, part = call_first(0, cp, (part, near, near_other), rows, kept)
    back_a = chip_permute(part, (3, 2, 0, 1), (3, 2, 0, 1))
    fin = (fin_near, fin_far)
    dq, part = call_stage(1, cp, (), fin, (slot1, slot2), rows, kept)
    back_b = chip_permute(part, (None, 0, 1, 2), (1, 2, 3, 0))
    dq, part = call_stage(2, cp, dq, fin, (slot3, slot1), rows, kept)
    back_c = chip_permute(part, (1, 2, 3, 0), (None, 0, 1, 2))
    dq, own = call_stage(3, cp, dq, fin, (kv, kv), rows, (*rows[4:], slot2, slot3, ds_near, ds_far))

    dq_other = core_swap(dq[1])
    token = jax.ShapeDtypeStruct((8, HDIM), jnp.float32)
    grad_query, done = simple(query_kernel, [jax.ShapeDtypeStruct(query.shape, query.dtype), token], dq[0], dq_other)
    total = jax.ShapeDtypeStruct(own.shape, own.dtype)
    half = simple(add_kernel, total, own, back_a, cost=BLOCK_COST)
    half = simple(add_kernel, total, half, back_b, cost=LONG_COST)
    half = simple(add_kernel, jax.ShapeDtypeStruct(kv.shape, kv.dtype), half, back_c)
    other = hd_swap(half)
    near = jax.ShapeDtypeStruct(keys.shape, keys.dtype)
    grad_keys, grad_values = simple(last_kernel, [near] * 2, half, other, done)
    return grad_query, grad_keys, grad_values


def solution(mesh):
    in_specs = (P("cp", "hd"), P("cp", None), P("cp", None), P("cp", "hd"), P("cp"))
    out_specs = (P("cp", "hd"), P("cp", None), P("cp", None))
    return jax.shard_map(body, mesh=mesh, in_specs=in_specs, out_specs=out_specs, check_vma=False)
```

```python
import functools
import math

import jax
import jax.numpy as jnp
from jax import lax
from jax.experimental import pallas as pl
from jax.experimental.pallas import tpu as pltpu
from jax.sharding import PartitionSpec as P

HDIM = 128
GROUP = 8
SCALE = 1.0 / math.sqrt(HDIM)
EXP_SCALE = SCALE * math.log2(math.e)
MASKED = -1e30
FLOOR = -1e29
KERNEL_VMEM = 16 * 2**20
KEYS = 512

NT = (((1,), (1,)), ((), ()))
NN = (((1,), (0,)), ((), ()))
TN = (((0,), (0,)), ((), ()))


def dot(a, b, dims):
    return lax.dot_general(a, b, dims, preferred_element_type=jnp.float32)


def chip_shift(array, even, odd):
    n = lax.axis_size("cp")
    pairs = [(i, i - i % GROUP + (i % GROUP + 2 * (odd if i % 2 else even)) % GROUP) for i in range(n)]
    return lax.ppermute(array, "cp", pairs)


def chip_permute(array, even, odd):
    n = lax.axis_size("cp")
    to = [(odd if i % 2 else even)[i % GROUP // 2] for i in range(n)]
    pairs = [(i, i - i % GROUP + 2 * to[i] + i % 2) for i in range(n) if to[i] is not None]
    return lax.ppermute(array, "cp", pairs)


def core_swap(array):
    n = lax.axis_size("cp")
    return lax.ppermute(array, "cp", [(i, i ^ 1) for i in range(n)])


def hd_swap(array):
    return lax.ppermute(array, "hd", [(0, 1), (1, 0)])


def masked_scores(k, q, starts, row_base, key_base, diagonal):
    s = dot(k, q, NT)
    key_pos = key_base + lax.broadcasted_iota(jnp.int32, s.shape, 0)
    allowed = key_pos >= starts
    if diagonal:
        row_pos = row_base + lax.broadcasted_iota(jnp.int32, s.shape, 1)
        allowed = allowed & (key_pos <= row_pos)
    return jnp.where(allowed, s, MASKED)


def slot_distance(slot, cp):
    return slot if slot < 2 else slot + lax.rem(cp, 2) * (5 - 2 * slot)


def stats_kernel(step, slot, groups, pos_ref, *refs):
    if step == 0:
        kv, q_own, g_own, st_own, stats, *copies = refs
        for src, dst in zip((q_own, g_own, st_own), copies):
            dst[...] = src[...]
        rows = ((q_own, g_own, st_own),)
    else:
        stats_in, *refs = refs
        if step == 1:
            own, *refs = refs
        else:
            refs = refs[2:]
        kv, q_own, q_sib, g_own, g_sib, st_own, st_sib, stats, *kept = refs
        rows = ((q_own, g_own, st_own), (q_sib, g_sib, st_sib))
    cp = pos_ref[0]
    in_group = lax.rem(cp, GROUP)
    size = kv.shape[1]
    base = 6 * groups[0]
    if step:
        stats[...] = stats_in[base : base + stats.shape[0], :]
    else:
        for at in range(0, 12, 3):
            stats[at : at + 1, :] = jnp.full((1, size), FLOOR)
            stats[at + 1 : at + 3, :] = jnp.zeros((2, size))
    chips = slot_distance(slot, cp)

    def work(kv, group, chips, keep):
        q, g, st = rows[group]
        key_base = (cp - 2 * chips) * size
        row_base = (cp if group == 0 else cp + 1 - 2 * lax.rem(cp, 2)) * size
        for head in range(2):
            cols = pl.ds(head * HDIM, HDIM)
            at = 3 * (2 * group + head) - base
            for first in range(0, size, KEYS):
                keys = pl.ds(first, KEYS)
                s = masked_scores(kv[0, keys], q[:, cols], st[...], row_base, key_base + first, step == 0)
                dp = dot(kv[1, keys], g[:, cols], NT)
                if keep:
                    kept[0][chips - 1, 2 * group + head, keys] = s
                    kept[1][chips - 1, 2 * group + head, keys] = dp
                m = stats[at : at + 1, :]
                new = jnp.maximum(m, jnp.max(s, axis=0, keepdims=True))
                p = jnp.exp2((s - new) * EXP_SCALE)
                f = jnp.exp2((m - new) * EXP_SCALE)
                stats[at : at + 1, :] = new
                stats[at + 1 : at + 2, :] = stats[at + 1 : at + 2, :] * f + jnp.sum(p, axis=0, keepdims=True)
                stats[at + 2 : at + 3, :] = stats[at + 2 : at + 3, :] * f + jnp.sum(p * dp, axis=0, keepdims=True)

    if step == 0:
        work(kv, 0, 0, False)
    if step == 1:
        pl.when(lax.rem(cp, 2) == 0)(lambda: work(own, 1, 0, False))
    if step:

        @pl.when(in_group >= 2 * chips)
        def _():
            for group in groups:
                work(kv, group, chips, True)


def merged(stats, other, at):
    m, m2 = stats[at : at + 1, :], other[at : at + 1, :]
    top = jnp.maximum(m, m2)
    f, f2 = jnp.exp2((m - top) * EXP_SCALE), jnp.exp2((m2 - top) * EXP_SCALE)
    total = stats[at + 1 : at + 2, :] * f + other[at + 1 : at + 2, :] * f2
    weighted = stats[at + 2 : at + 3, :] * f + other[at + 2 : at + 3, :] * f2
    return top * EXP_SCALE + jnp.log2(total), weighted / total


def stage_distance(stage, cp):
    odd = lax.rem(cp, 2)
    return (2, 1 + 2 * odd, 3 - 2 * odd, 0)[stage]


def add_grads(q, g, s, dp, fin, at, acc, cols):
    p = jnp.exp2(s * EXP_SCALE - fin[at : at + 1, :])
    ds = (p * (dp - fin[at + 1 : at + 2, :])).astype(jnp.bfloat16)
    acc[0] += dot(ds, q[:, cols], NN)
    acc[1] += dot(p.astype(jnp.bfloat16), g[:, cols], NN)
    return ds


def first_kernel(group, pos_ref, *refs):
    if group == 0:
        acc_in, *refs = refs
    stats, other, q, g, kept0, kept1, kept, fin, *refs = refs
    acc = refs[-1]
    for head in range(2):
        log_sum, delta = merged(stats, other, 3 * head)
        fin[2 * head : 2 * head + 1, :] = log_sum
        fin[2 * head + 1 : 2 * head + 2, :] = delta
    acc[...] = acc_in[...] if group == 0 else jnp.zeros_like(acc)
    cp = pos_ref[0]
    chips = stage_distance(0, cp)

    @pl.when(lax.rem(cp, GROUP) >= 2 * chips)
    def _():
        for head in range(2):
            at = 2 * group + head
            cols = pl.ds(head * HDIM, HDIM)
            kept[head] = add_grads(q, g, kept0[chips - 1, at], kept1[chips - 1, at], fin, 2 * head, acc, cols)

    if group == 0:
        refs[0][...] = acc[...].astype(jnp.bfloat16)


def grads_kernel(stage, pos_ref, *refs):
    if stage > 1:
        dq_in, refs = refs[:2], refs[2:]
    (fin_own, fin_sib), refs = refs[:2], refs[2:]
    even, odd, q_own, q_sib, g_own, g_sib, kept0, kept1, *refs = refs
    if stage == 3:
        first_even, first_odd, *first, dq_own, dq_sib, dkv, acc = refs
    else:
        dq_own, dq_sib, dkv, acc = refs
    cp = pos_ref[0]
    in_group = lax.rem(cp, GROUP)
    even_core = lax.rem(cp, 2) == 0
    size = q_own.shape[0]
    acc[...] = jnp.zeros_like(acc)
    for i, dq in enumerate((dq_own, dq_sib)):
        dq[...] = dq_in[i][...] if stage > 1 else jnp.zeros_like(dq)
    chips = stage_distance(stage, cp)
    k = even[0] if stage == 3 else jnp.where(even_core, even[0], odd[0])
    k_t = k.T
    groups = ((q_own, g_own, fin_own, dq_own), (q_sib, g_sib, fin_sib, dq_sib))
    for group, (q, g, fin, dq) in enumerate(groups):

        def work(group=group, q=q, g=g, fin=fin, dq=dq):
            for head in range(2):
                cols = pl.ds(head * HDIM, HDIM)
                if stage < 3:
                    s = kept0[chips - 1, 2 * group + head]
                    dp = kept1[chips - 1, 2 * group + head]
                else:
                    starts = (kept0, kept1)[group][...]
                    s = masked_scores(k, q[:, cols], starts, (cp + group) * size, cp * size, group == 0)
                    dp = dot(even[1], g[:, cols], NT)
                ds = add_grads(q, g, s, dp, fin, 2 * head, acc, cols)
                dq[cols, :] += dot(k_t, ds, NN)

        if stage == 3 and group == 0:
            work()
        elif stage == 3:
            pl.when(even_core)(work)
        else:
            pl.when(in_group >= 2 * chips)(work)
    dkv[...] = acc[...].astype(dkv.dtype)
    if stage == 3:

        @pl.when(in_group >= 2 * stage_distance(0, cp))
        def _():
            first_t = jnp.where(even_core, first_even[0], first_odd[0]).T
            for ds, dq in zip(first, (dq_own, dq_sib)):
                for head in range(2):
                    dq[pl.ds(head * HDIM, HDIM), :] += dot(first_t, ds[head], NN)


def query_kernel(mine, other, out, done):
    done[...] = jnp.zeros_like(done)
    out[...] = ((mine[...] + other[...]) * SCALE).T.astype(out.dtype)


def add_kernel(total, part, out):
    out[...] = (total[...] + part[...].astype(jnp.float32)).astype(out.dtype)


def last_kernel(mine, other, _, grad_keys, grad_values):
    total = mine[...].astype(jnp.float32) + other[...].astype(jnp.float32)
    grad_keys[...] = (total[0] * SCALE).astype(grad_keys.dtype)
    grad_values[...] = total[1].astype(grad_values.dtype)


VM = pl.BlockSpec(memory_space=pltpu.VMEM)
SM = pl.BlockSpec(memory_space=pltpu.SMEM)


BLOCK_COST = pl.CostEstimate(flops=10 * 512 * 512 * 128 // 10, bytes_accessed=2**10, transcendentals=0)
LONG_COST = pl.CostEstimate(flops=40 * 10 * 512 * 512 * 128, bytes_accessed=2**20, transcendentals=0)
NO_COST = pl.CostEstimate(flops=0, bytes_accessed=2**10, transcendentals=0)


def simple(kernel, out, *args, cost=NO_COST):
    return pl.pallas_call(
        kernel,
        out_shape=out,
        in_specs=[VM] * len(args),
        out_specs=jax.tree.map(lambda _: VM, out),
        compiler_params=pltpu.CompilerParams(vmem_limit_bytes=8 * 2**20),
        cost_estimate=cost,
    )(*args)


def call_stats(step, slot, cp, before, kv, rows, groups=(0, 1)):
    size = kv.shape[1]
    out = [jax.ShapeDtypeStruct((6 * len(groups), size), jnp.float32)]
    if step:
        out += [jax.ShapeDtypeStruct((3, 4, size, size), jnp.float32)] * 2
    else:
        out += [jax.ShapeDtypeStruct(a.shape, a.dtype) for a in rows]
    in_specs = [SM] + [VM] * (len(before) + 1 + len(rows))
    if step > 1:
        in_specs[2:4] = [pl.BlockSpec(memory_space=pl.ANY)] * 2
    return pl.pallas_call(
        functools.partial(stats_kernel, step, slot, groups),
        out_shape=out,
        in_specs=in_specs,
        out_specs=[VM] * len(out),
        input_output_aliases={2: 1, 3: 2} if step > 1 else {},
        compiler_params=pltpu.CompilerParams(vmem_limit_bytes=KERNEL_VMEM),
        cost_estimate=NO_COST,
        name="stats",
    )(cp, *before, kv, *rows)


def call_grads(kernel, cp, out, args, cost, scratch=()):
    return pl.pallas_call(
        kernel,
        out_shape=out,
        in_specs=[SM] + [VM] * len(args),
        out_specs=[VM] * len(out),
        scratch_shapes=scratch,
        compiler_params=pltpu.CompilerParams(vmem_limit_bytes=KERNEL_VMEM),
        cost_estimate=cost,
        name="grads",
    )(cp, *args)


def call_first(group, cp, before, rows, kept):
    size = rows[0].shape[0]
    total = (2, size, HDIM)
    out = [jax.ShapeDtypeStruct((2, size, size), jnp.bfloat16), jax.ShapeDtypeStruct((4, size), jnp.float32)]
    out.append(jax.ShapeDtypeStruct(total, jnp.float32 if group else jnp.bfloat16))
    scratch = [] if group else [pltpu.VMEM(total, jnp.float32)]
    args = (*before, rows[group], rows[2 + group], *kept)
    return call_grads(functools.partial(first_kernel, group), cp, out, args, NO_COST if group else BLOCK_COST, scratch)


def call_stage(stage, cp, dq, fin, blocks, rows, kept):
    size = rows[0].shape[0]
    total = (2, size, HDIM)
    out = [jax.ShapeDtypeStruct((2 * HDIM, size), jnp.float32)] * 2
    out.append(jax.ShapeDtypeStruct(total, jnp.float32 if stage == 3 else jnp.bfloat16))
    args = (*dq, *fin, *blocks, *rows[:4], *kept)
    cost = NO_COST if stage == 3 else BLOCK_COST
    *dq, part = call_grads(functools.partial(grads_kernel, stage), cp, out, args, cost, [pltpu.VMEM(total, jnp.float32)])
    return dq, part


def body(query, keys, values, grad_out, doc_start):
    size = query.shape[0]
    position = lax.axis_index("cp").astype(jnp.int32)
    cp = position.reshape(1)
    kv = jnp.where(lax.broadcasted_iota(jnp.int32, (2, *keys.shape), 0) == 0, keys[None], values[None])
    slot1 = chip_shift(kv, 1, 1)
    slot2 = chip_permute(kv, (2, 3, 1, 0), (3, 0, 1, 2))
    slot3 = chip_permute(kv, (3, 0, 1, 2), (2, 3, 1, 0))
    starts = doc_start.reshape(1, size)
    kv, near_query, near_grad = lax.optimization_barrier((kv, query, grad_out))
    far_query, near_starts = lax.optimization_barrier((core_swap(near_query), starts))
    far_grad, far_starts = core_swap(near_grad), core_swap(near_starts)

    stats, *own_rows = call_stats(0, 0, cp, (), kv, (query, grad_out, starts))
    rows = (own_rows[0], far_query, own_rows[1], far_grad, own_rows[2], far_starts)
    before = call_stats(1, 1, cp, (stats, kv), slot1, rows)
    before = call_stats(2, 2, cp, before, slot2, rows)
    stats = before[0]
    near, *kept = call_stats(3, 3, cp, before, slot3, rows, (0,))
    far_other = core_swap(near)
    far, *kept = call_stats(3, 3, cp, (stats, *kept), slot3, rows, (1,))
    near_other = core_swap(far)

    ds_far, fin_far, part = call_first(1, cp, (far, far_other), rows, kept)
    ds_near, fin_near, part = call_first(0, cp, (part, near, near_other), rows, kept)
    back_a = chip_permute(part, (3, 2, 0, 1), (3, 2, 0, 1))
    fin = (fin_near, fin_far)
    dq, part = call_stage(1, cp, (), fin, (slot1, slot2), rows, kept)
    back_b = chip_permute(part, (None, 0, 1, 2), (1, 2, 3, 0))
    dq, part = call_stage(2, cp, dq, fin, (slot3, slot1), rows, kept)
    back_c = chip_permute(part, (1, 2, 3, 0), (None, 0, 1, 2))
    dq, own = call_stage(3, cp, dq, fin, (kv, kv), rows, (*rows[4:], slot2, slot3, ds_near, ds_far))

    dq_other = core_swap(dq[1])
    token = jax.ShapeDtypeStruct((8, HDIM), jnp.float32)
    grad_query, done = simple(query_kernel, [jax.ShapeDtypeStruct(query.shape, query.dtype), token], dq[0], dq_other)
    total = jax.ShapeDtypeStruct(own.shape, own.dtype)
    half = simple(add_kernel, total, own, back_a, cost=BLOCK_COST)
    half = simple(add_kernel, total, half, back_b, cost=LONG_COST)
    half = simple(add_kernel, jax.ShapeDtypeStruct(kv.shape, kv.dtype), half, back_c)
    other = hd_swap(half)
    near = jax.ShapeDtypeStruct(keys.shape, keys.dtype)
    grad_keys, grad_values = simple(last_kernel, [near] * 2, half, other, done)
    return grad_query, grad_keys, grad_values


def solution(mesh):
    in_specs = (P("cp", "hd"), P("cp", None), P("cp", None), P("cp", "hd"), P("cp"))
    out_specs = (P("cp", "hd"), P("cp", None), P("cp", None))
    return jax.shard_map(body, mesh=mesh, in_specs=in_specs, out_specs=out_specs, check_vma=False)
```

```python
import functools
import math

import jax
import jax.numpy as jnp
from jax import lax
from jax.experimental import pallas as pl
from jax.experimental.pallas import tpu as pltpu
from jax.sharding import PartitionSpec as P

HDIM = 128
GROUP = 8
SCALE = 1.0 / math.sqrt(HDIM)
EXP_SCALE = SCALE * math.log2(math.e)
MASKED = -1e30
FLOOR = -1e29
KERNEL_VMEM = 16 * 2**20
KEYS = 512

NT = (((1,), (1,)), ((), ()))
NN = (((1,), (0,)), ((), ()))
TN = (((0,), (0,)), ((), ()))


def dot(a, b, dims):
    return lax.dot_general(a, b, dims, preferred_element_type=jnp.float32)


def chip_shift(array, even, odd):
    n = lax.axis_size("cp")
    pairs = [(i, i - i % GROUP + (i % GROUP + 2 * (odd if i % 2 else even)) % GROUP) for i in range(n)]
    return lax.ppermute(array, "cp", pairs)


def chip_permute(array, even, odd):
    n = lax.axis_size("cp")
    to = [(odd if i % 2 else even)[i % GROUP // 2] for i in range(n)]
    pairs = [(i, i - i % GROUP + 2 * to[i] + i % 2) for i in range(n) if to[i] is not None]
    return lax.ppermute(array, "cp", pairs)


def core_swap(array):
    n = lax.axis_size("cp")
    return lax.ppermute(array, "cp", [(i, i ^ 1) for i in range(n)])


def hd_swap(array):
    return lax.ppermute(array, "hd", [(0, 1), (1, 0)])


def masked_scores(k, q, starts, row_base, key_base, diagonal):
    s = dot(k, q, NT)
    key_pos = key_base + lax.broadcasted_iota(jnp.int32, s.shape, 0)
    allowed = key_pos >= starts
    if diagonal:
        row_pos = row_base + lax.broadcasted_iota(jnp.int32, s.shape, 1)
        allowed = allowed & (key_pos <= row_pos)
    return jnp.where(allowed, s, MASKED)


def slot_distance(slot, cp):
    return slot if slot < 2 else slot + lax.rem(cp, 2) * (5 - 2 * slot)


def stats_kernel(step, slot, groups, pos_ref, *refs):
    if step == 0:
        kv, q_own, g_own, st_own, stats, *copies = refs
        for src, dst in zip((q_own, g_own, st_own), copies):
            dst[...] = src[...]
        rows = ((q_own, g_own, st_own),)
    else:
        stats_in, *refs = refs
        if step == 1:
            own, *refs = refs
        else:
            refs = refs[2:]
        kv, q_own, q_sib, g_own, g_sib, st_own, st_sib, stats, *kept = refs
        rows = ((q_own, g_own, st_own), (q_sib, g_sib, st_sib))
    cp = pos_ref[0]
    in_group = lax.rem(cp, GROUP)
    size = kv.shape[1]
    base = 6 * groups[0]
    if step:
        stats[...] = stats_in[base : base + stats.shape[0], :]
    else:
        for at in range(0, 12, 3):
            stats[at : at + 1, :] = jnp.full((1, size), FLOOR)
            stats[at + 1 : at + 3, :] = jnp.zeros((2, size))
    chips = slot_distance(slot, cp)

    def work(kv, group, chips, keep):
        q, g, st = rows[group]
        key_base = (cp - 2 * chips) * size
        row_base = (cp if group == 0 else cp + 1 - 2 * lax.rem(cp, 2)) * size
        for head in range(2):
            cols = pl.ds(head * HDIM, HDIM)
            at = 3 * (2 * group + head) - base
            for first in range(0, size, KEYS):
                keys = pl.ds(first, KEYS)
                s = masked_scores(kv[0, keys], q[:, cols], st[...], row_base, key_base + first, step == 0)
                dp = dot(kv[1, keys], g[:, cols], NT)
                if keep:
                    kept[0][chips - 1, 2 * group + head, keys] = s
                    kept[1][chips - 1, 2 * group + head, keys] = dp
                m = stats[at : at + 1, :]
                new = jnp.maximum(m, jnp.max(s, axis=0, keepdims=True))
                p = jnp.exp2((s - new) * EXP_SCALE)
                f = jnp.exp2((m - new) * EXP_SCALE)
                stats[at : at + 1, :] = new
                stats[at + 1 : at + 2, :] = stats[at + 1 : at + 2, :] * f + jnp.sum(p, axis=0, keepdims=True)
                stats[at + 2 : at + 3, :] = stats[at + 2 : at + 3, :] * f + jnp.sum(p * dp, axis=0, keepdims=True)

    if step == 0:
        work(kv, 0, 0, False)
    if step == 1:
        pl.when(lax.rem(cp, 2) == 0)(lambda: work(own, 1, 0, False))
    if step:

        @pl.when(in_group >= 2 * chips)
        def _():
            for group in groups:
                work(kv, group, chips, True)


def merged(stats, other, at):
    m, m2 = stats[at : at + 1, :], other[at : at + 1, :]
    top = jnp.maximum(m, m2)
    f, f2 = jnp.exp2((m - top) * EXP_SCALE), jnp.exp2((m2 - top) * EXP_SCALE)
    total = stats[at + 1 : at + 2, :] * f + other[at + 1 : at + 2, :] * f2
    weighted = stats[at + 2 : at + 3, :] * f + other[at + 2 : at + 3, :] * f2
    return top * EXP_SCALE + jnp.log2(total), weighted / total


def stage_distance(stage, cp):
    odd = lax.rem(cp, 2)
    return (2, 1 + 2 * odd, 3 - 2 * odd, 0)[stage]


def add_grads(q, g, s, dp, fin, at, acc, cols):
    p = jnp.exp2(s * EXP_SCALE - fin[at : at + 1, :])
    ds = (p * (dp - fin[at + 1 : at + 2, :])).astype(jnp.bfloat16)
    acc[0] += dot(ds, q[:, cols], NN)
    acc[1] += dot(p.astype(jnp.bfloat16), g[:, cols], NN)
    return ds


def first_kernel(group, pos_ref, *refs):
    if group == 0:
        acc_in, *refs = refs
    stats, other, q, g, kept0, kept1, kept, fin, *refs = refs
    acc = refs[-1]
    for head in range(2):
        log_sum, delta = merged(stats, other, 3 * head)
        fin[2 * head : 2 * head + 1, :] = log_sum
        fin[2 * head + 1 : 2 * head + 2, :] = delta
    acc[...] = acc_in[...] if group == 0 else jnp.zeros_like(acc)
    cp = pos_ref[0]
    chips = stage_distance(0, cp)

    @pl.when(lax.rem(cp, GROUP) >= 2 * chips)
    def _():
        for head in range(2):
            at = 2 * group + head
            cols = pl.ds(head * HDIM, HDIM)
            kept[head] = add_grads(q, g, kept0[chips - 1, at], kept1[chips - 1, at], fin, 2 * head, acc, cols)

    if group == 0:
        refs[0][...] = acc[...].astype(jnp.bfloat16)


def grads_kernel(stage, pos_ref, *refs):
    if stage > 1:
        dq_in, refs = refs[:2], refs[2:]
    (fin_own, fin_sib), refs = refs[:2], refs[2:]
    even, odd, q_own, q_sib, g_own, g_sib, kept0, kept1, *refs = refs
    if stage == 3:
        first_even, first_odd, *first, dq_own, dq_sib, dkv, acc = refs
    else:
        dq_own, dq_sib, dkv, acc = refs
    cp = pos_ref[0]
    in_group = lax.rem(cp, GROUP)
    even_core = lax.rem(cp, 2) == 0
    size = q_own.shape[0]
    acc[...] = jnp.zeros_like(acc)
    for i, dq in enumerate((dq_own, dq_sib)):
        dq[...] = dq_in[i][...] if stage > 1 else jnp.zeros_like(dq)
    chips = stage_distance(stage, cp)
    k = even[0] if stage == 3 else jnp.where(even_core, even[0], odd[0])
    k_t = k.T
    groups = ((q_own, g_own, fin_own, dq_own), (q_sib, g_sib, fin_sib, dq_sib))
    for group, (q, g, fin, dq) in enumerate(groups):

        def work(group=group, q=q, g=g, fin=fin, dq=dq):
            for head in range(2):
                cols = pl.ds(head * HDIM, HDIM)
                if stage < 3:
                    s = kept0[chips - 1, 2 * group + head]
                    dp = kept1[chips - 1, 2 * group + head]
                else:
                    starts = (kept0, kept1)[group][...]
                    s = masked_scores(k, q[:, cols], starts, (cp + group) * size, cp * size, group == 0)
                    dp = dot(even[1], g[:, cols], NT)
                ds = add_grads(q, g, s, dp, fin, 2 * head, acc, cols)
                dq[cols, :] += dot(k_t, ds, NN)

        if stage == 3 and group == 0:
            work()
        elif stage == 3:
            pl.when(even_core)(work)
        else:
            pl.when(in_group >= 2 * chips)(work)
    dkv[...] = acc[...].astype(dkv.dtype)
    if stage == 3:

        @pl.when(in_group >= 2 * stage_distance(0, cp))
        def _():
            first_t = jnp.where(even_core, first_even[0], first_odd[0]).T
            for ds, dq in zip(first, (dq_own, dq_sib)):
                for head in range(2):
                    dq[pl.ds(head * HDIM, HDIM), :] += dot(first_t, ds[head], NN)


def query_kernel(mine, other, out, done):
    done[...] = jnp.zeros_like(done)
    out[...] = ((mine[...] + other[...]) * SCALE).T.astype(out.dtype)


def add_kernel(total, part, out):
    out[...] = (total[...] + part[...].astype(jnp.float32)).astype(out.dtype)


def last_kernel(mine, other, _, grad_keys, grad_values):
    total = mine[...].astype(jnp.float32) + other[...].astype(jnp.float32)
    grad_keys[...] = (total[0] * SCALE).astype(grad_keys.dtype)
    grad_values[...] = total[1].astype(grad_values.dtype)


VM = pl.BlockSpec(memory_space=pltpu.VMEM)
SM = pl.BlockSpec(memory_space=pltpu.SMEM)


BLOCK_COST = pl.CostEstimate(flops=10 * 512 * 512 * 128 // 10, bytes_accessed=2**10, transcendentals=0)
LONG_COST = pl.CostEstimate(flops=40 * 10 * 512 * 512 * 128, bytes_accessed=2**20, transcendentals=0)
NO_COST = pl.CostEstimate(flops=0, bytes_accessed=2**10, transcendentals=0)


def simple(kernel, out, *args, cost=NO_COST):
    return pl.pallas_call(
        kernel,
        out_shape=out,
        in_specs=[VM] * len(args),
        out_specs=jax.tree.map(lambda _: VM, out),
        compiler_params=pltpu.CompilerParams(vmem_limit_bytes=8 * 2**20),
        cost_estimate=cost,
    )(*args)


def call_stats(step, slot, cp, before, kv, rows, groups=(0, 1)):
    size = kv.shape[1]
    out = [jax.ShapeDtypeStruct((6 * len(groups), size), jnp.float32)]
    if step:
        out += [jax.ShapeDtypeStruct((3, 4, size, size), jnp.float32)] * 2
    else:
        out += [jax.ShapeDtypeStruct(a.shape, a.dtype) for a in rows]
    in_specs = [SM] + [VM] * (len(before) + 1 + len(rows))
    if step > 1:
        in_specs[2:4] = [pl.BlockSpec(memory_space=pl.ANY)] * 2
    return pl.pallas_call(
        functools.partial(stats_kernel, step, slot, groups),
        out_shape=out,
        in_specs=in_specs,
        out_specs=[VM] * len(out),
        input_output_aliases={2: 1, 3: 2} if step > 1 else {},
        compiler_params=pltpu.CompilerParams(vmem_limit_bytes=KERNEL_VMEM),
        cost_estimate=NO_COST,
        name="stats",
    )(cp, *before, kv, *rows)


def call_grads(kernel, cp, out, args, cost, scratch=()):
    return pl.pallas_call(
        kernel,
        out_shape=out,
        in_specs=[SM] + [VM] * len(args),
        out_specs=[VM] * len(out),
        scratch_shapes=scratch,
        compiler_params=pltpu.CompilerParams(vmem_limit_bytes=KERNEL_VMEM),
        cost_estimate=cost,
        name="grads",
    )(cp, *args)


def call_first(group, cp, before, rows, kept):
    size = rows[0].shape[0]
    total = (2, size, HDIM)
    out = [jax.ShapeDtypeStruct((2, size, size), jnp.bfloat16), jax.ShapeDtypeStruct((4, size), jnp.float32)]
    out.append(jax.ShapeDtypeStruct(total, jnp.float32 if group else jnp.bfloat16))
    scratch = [] if group else [pltpu.VMEM(total, jnp.float32)]
    args = (*before, rows[group], rows[2 + group], *kept)
    return call_grads(functools.partial(first_kernel, group), cp, out, args, NO_COST if group else BLOCK_COST, scratch)


def call_stage(stage, cp, dq, fin, blocks, rows, kept):
    size = rows[0].shape[0]
    total = (2, size, HDIM)
    out = [jax.ShapeDtypeStruct((2 * HDIM, size), jnp.float32)] * 2
    out.append(jax.ShapeDtypeStruct(total, jnp.float32 if stage == 3 else jnp.bfloat16))
    args = (*dq, *fin, *blocks, *rows[:4], *kept)
    cost = NO_COST if stage == 3 else BLOCK_COST
    *dq, part = call_grads(functools.partial(grads_kernel, stage), cp, out, args, cost, [pltpu.VMEM(total, jnp.float32)])
    return dq, part


def body(query, keys, values, grad_out, doc_start):
    size = query.shape[0]
    position = lax.axis_index("cp").astype(jnp.int32)
    cp = position.reshape(1)
    kv = jnp.where(lax.broadcasted_iota(jnp.int32, (2, *keys.shape), 0) == 0, keys[None], values[None])
    slot1 = chip_shift(kv, 1, 1)
    slot2 = chip_permute(kv, (2, 3, 0, 1), (3, 0, 1, 2))
    slot3 = chip_permute(kv, (3, 0, 1, 2), (2, 3, 0, 1))
    starts = doc_start.reshape(1, size)
    kv, near_query, near_grad = lax.optimization_barrier((kv, query, grad_out))
    far_query, near_starts = lax.optimization_barrier((core_swap(near_query), starts))
    far_grad, far_starts = core_swap(near_grad), core_swap(near_starts)

    stats, *own_rows = call_stats(0, 0, cp, (), kv, (query, grad_out, starts))
    rows = (own_rows[0], far_query, own_rows[1], far_grad, own_rows[2], far_starts)
    before = call_stats(1, 1, cp, (stats, kv), slot1, rows)
    before = call_stats(2, 2, cp, before, slot2, rows)
    stats = before[0]
    near, *kept = call_stats(3, 3, cp, before, slot3, rows, (0,))
    far_other = core_swap(near)
    far, *kept = call_stats(3, 3, cp, (stats, *kept), slot3, rows, (1,))
    near_other = core_swap(far)

    ds_far, fin_far, part = call_first(1, cp, (far, far_other), rows, kept)
    ds_near, fin_near, part = call_first(0, cp, (part, near, near_other), rows, kept)
    back_a = chip_permute(part, (3, 2, 0, 1), (3, 2, 0, 1))
    fin = (fin_near, fin_far)
    dq, part = call_stage(1, cp, (), fin, (slot1, slot2), rows, kept)
    back_b = chip_permute(part, (None, 0, 1, 2), (None, 2, 3, 0))
    dq, part = call_stage(2, cp, dq, fin, (slot3, slot1), rows, kept)
    back_c = chip_permute(part, (None, 2, 3, 0), (None, 0, 1, 2))
    dq, own = call_stage(3, cp, dq, fin, (kv, kv), rows, (*rows[4:], slot2, slot3, ds_near, ds_far))

    dq_other = core_swap(dq[1])
    token = jax.ShapeDtypeStruct((8, HDIM), jnp.float32)
    grad_query, done = simple(query_kernel, [jax.ShapeDtypeStruct(query.shape, query.dtype), token], dq[0], dq_other)
    total = jax.ShapeDtypeStruct(own.shape, own.dtype)
    half = simple(add_kernel, total, own, back_a, cost=BLOCK_COST)
    half = simple(add_kernel, total, half, back_b, cost=LONG_COST)
    half = simple(add_kernel, jax.ShapeDtypeStruct(kv.shape, kv.dtype), half, back_c)
    other = hd_swap(half)
    near = jax.ShapeDtypeStruct(keys.shape, keys.dtype)
    grad_keys, grad_values = simple(last_kernel, [near] * 2, half, other, done)
    return grad_query, grad_keys, grad_values


def solution(mesh):
    in_specs = (P("cp", "hd"), P("cp", None), P("cp", None), P("cp", "hd"), P("cp"))
    out_specs = (P("cp", "hd"), P("cp", None), P("cp", None))
    return jax.shard_map(body, mesh=mesh, in_specs=in_specs, out_specs=out_specs, check_vma=False)
```

```python
import functools
import math

import jax
import jax.numpy as jnp
from jax import lax
from jax.experimental import pallas as pl
from jax.experimental.pallas import tpu as pltpu
from jax.sharding import PartitionSpec as P

HDIM = 128
GROUP = 8
SCALE = 1.0 / math.sqrt(HDIM)
EXP_SCALE = SCALE * math.log2(math.e)
MASKED = -1e30
FLOOR = -1e29
KERNEL_VMEM = 16 * 2**20
KEYS = 512

NT = (((1,), (1,)), ((), ()))
NN = (((1,), (0,)), ((), ()))
TN = (((0,), (0,)), ((), ()))


def dot(a, b, dims):
    return lax.dot_general(a, b, dims, preferred_element_type=jnp.float32)


def chip_shift(array, even, odd):
    n = lax.axis_size("cp")
    pairs = [(i, i - i % GROUP + (i % GROUP + 2 * (odd if i % 2 else even)) % GROUP) for i in range(n)]
    return lax.ppermute(array, "cp", pairs)


def chip_permute(array, even, odd):
    n = lax.axis_size("cp")
    to = [(odd if i % 2 else even)[i % GROUP // 2] for i in range(n)]
    pairs = [(i, i - i % GROUP + 2 * to[i] + i % 2) for i in range(n) if to[i] is not None]
    return lax.ppermute(array, "cp", pairs)


def core_swap(array):
    n = lax.axis_size("cp")
    return lax.ppermute(array, "cp", [(i, i ^ 1) for i in range(n)])


def hd_swap(array):
    return lax.ppermute(array, "hd", [(0, 1), (1, 0)])


def masked_scores(k, q, starts, row_base, key_base, diagonal):
    s = dot(k, q, NT)
    key_pos = key_base + lax.broadcasted_iota(jnp.int32, s.shape, 0)
    allowed = key_pos >= starts
    if diagonal:
        row_pos = row_base + lax.broadcasted_iota(jnp.int32, s.shape, 1)
        allowed = allowed & (key_pos <= row_pos)
    return jnp.where(allowed, s, MASKED)


def slot_distance(slot, cp):
    return slot if slot < 2 else slot + lax.rem(cp, 2) * (5 - 2 * slot)


def stats_kernel(step, slot, groups, pos_ref, *refs):
    if step == 0:
        kv, q_own, g_own, st_own, stats, *copies = refs
        for src, dst in zip((q_own, g_own, st_own), copies):
            dst[...] = src[...]
        rows = ((q_own, g_own, st_own),)
    else:
        stats_in, *refs = refs
        if step == 1:
            own, *refs = refs
        else:
            refs = refs[2:]
        kv, q_own, q_sib, g_own, g_sib, st_own, st_sib, stats, *kept = refs
        rows = ((q_own, g_own, st_own), (q_sib, g_sib, st_sib))
    cp = pos_ref[0]
    in_group = lax.rem(cp, GROUP)
    size = kv.shape[1]
    base = 6 * groups[0]
    if step:
        stats[...] = stats_in[base : base + stats.shape[0], :]
    else:
        for at in range(0, 12, 3):
            stats[at : at + 1, :] = jnp.full((1, size), FLOOR)
            stats[at + 1 : at + 3, :] = jnp.zeros((2, size))
    chips = slot_distance(slot, cp)

    def work(kv, group, chips, keep):
        q, g, st = rows[group]
        key_base = (cp - 2 * chips) * size
        row_base = (cp if group == 0 else cp + 1 - 2 * lax.rem(cp, 2)) * size
        for head in range(2):
            cols = pl.ds(head * HDIM, HDIM)
            at = 3 * (2 * group + head) - base
            for first in range(0, size, KEYS):
                keys = pl.ds(first, KEYS)
                s = masked_scores(kv[0, keys], q[:, cols], st[...], row_base, key_base + first, step == 0)
                dp = dot(kv[1, keys], g[:, cols], NT)
                if keep:
                    kept[0][chips - 1, 2 * group + head, keys] = s
                    kept[1][chips - 1, 2 * group + head, keys] = dp
                m = stats[at : at + 1, :]
                new = jnp.maximum(m, jnp.max(s, axis=0, keepdims=True))
                p = jnp.exp2((s - new) * EXP_SCALE)
                f = jnp.exp2((m - new) * EXP_SCALE)
                stats[at : at + 1, :] = new
                stats[at + 1 : at + 2, :] = stats[at + 1 : at + 2, :] * f + jnp.sum(p, axis=0, keepdims=True)
                stats[at + 2 : at + 3, :] = stats[at + 2 : at + 3, :] * f + jnp.sum(p * dp, axis=0, keepdims=True)

    if step == 0:
        work(kv, 0, 0, False)
    if step == 1:
        pl.when(lax.rem(cp, 2) == 0)(lambda: work(own, 1, 0, False))
    if step:

        @pl.when(in_group >= 2 * chips)
        def _():
            for group in groups:
                work(kv, group, chips, True)


def merged(stats, other, at):
    m, m2 = stats[at : at + 1, :], other[at : at + 1, :]
    top = jnp.maximum(m, m2)
    f, f2 = jnp.exp2((m - top) * EXP_SCALE), jnp.exp2((m2 - top) * EXP_SCALE)
    total = stats[at + 1 : at + 2, :] * f + other[at + 1 : at + 2, :] * f2
    weighted = stats[at + 2 : at + 3, :] * f + other[at + 2 : at + 3, :] * f2
    return top * EXP_SCALE + jnp.log2(total), weighted / total


def stage_distance(stage, cp):
    odd = lax.rem(cp, 2)
    return (2, 1 + 2 * odd, 3 - 2 * odd, 0)[stage]


def add_grads(q, g, s, dp, fin, at, acc, cols):
    p = jnp.exp2(s * EXP_SCALE - fin[at : at + 1, :])
    ds = (p * (dp - fin[at + 1 : at + 2, :])).astype(jnp.bfloat16)
    acc[0] += dot(ds, q[:, cols], NN)
    acc[1] += dot(p.astype(jnp.bfloat16), g[:, cols], NN)
    return ds


def first_kernel(group, pos_ref, *refs):
    if group == 0:
        acc_in, *refs = refs
    stats, other, q, g, kept0, kept1, kept, fin, *refs = refs
    acc = refs[-1]
    for head in range(2):
        log_sum, delta = merged(stats, other, 3 * head)
        fin[2 * head : 2 * head + 1, :] = log_sum
        fin[2 * head + 1 : 2 * head + 2, :] = delta
    acc[...] = acc_in[...] if group == 0 else jnp.zeros_like(acc)
    cp = pos_ref[0]
    chips = stage_distance(0, cp)

    @pl.when(lax.rem(cp, GROUP) >= 2 * chips)
    def _():
        for head in range(2):
            at = 2 * group + head
            cols = pl.ds(head * HDIM, HDIM)
            kept[head] = add_grads(q, g, kept0[chips - 1, at], kept1[chips - 1, at], fin, 2 * head, acc, cols)

    if group == 0:
        refs[0][...] = acc[...].astype(jnp.bfloat16)


def grads_kernel(stage, pos_ref, *refs):
    if stage > 1:
        dq_in, refs = refs[:2], refs[2:]
    (fin_own, fin_sib), refs = refs[:2], refs[2:]
    even, odd, q_own, q_sib, g_own, g_sib, kept0, kept1, *refs = refs
    if stage == 3:
        first_even, first_odd, *first, dq_own, dq_sib, dkv, acc = refs
    else:
        dq_own, dq_sib, dkv, acc = refs
    cp = pos_ref[0]
    in_group = lax.rem(cp, GROUP)
    even_core = lax.rem(cp, 2) == 0
    size = q_own.shape[0]
    acc[...] = jnp.zeros_like(acc)
    for i, dq in enumerate((dq_own, dq_sib)):
        dq[...] = dq_in[i][...] if stage > 1 else jnp.zeros_like(dq)
    chips = stage_distance(stage, cp)
    k = even[0] if stage == 3 else jnp.where(even_core, even[0], odd[0])
    k_t = k.T
    groups = ((q_own, g_own, fin_own, dq_own), (q_sib, g_sib, fin_sib, dq_sib))
    for group, (q, g, fin, dq) in enumerate(groups):

        def work(group=group, q=q, g=g, fin=fin, dq=dq):
            for head in range(2):
                cols = pl.ds(head * HDIM, HDIM)
                if stage < 3:
                    s = kept0[chips - 1, 2 * group + head]
                    dp = kept1[chips - 1, 2 * group + head]
                else:
                    starts = (kept0, kept1)[group][...]
                    s = masked_scores(k, q[:, cols], starts, (cp + group) * size, cp * size, group == 0)
                    dp = dot(even[1], g[:, cols], NT)
                ds = add_grads(q, g, s, dp, fin, 2 * head, acc, cols)
                dq[cols, :] += dot(k_t, ds, NN)

        if stage == 3 and group == 0:
            work()
        elif stage == 3:
            pl.when(even_core)(work)
        else:
            pl.when(in_group >= 2 * chips)(work)
    dkv[...] = acc[...].astype(dkv.dtype)
    if stage == 3:

        @pl.when(in_group >= 2 * stage_distance(0, cp))
        def _():
            first_t = jnp.where(even_core, first_even[0], first_odd[0]).T
            for ds, dq in zip(first, (dq_own, dq_sib)):
                for head in range(2):
                    dq[pl.ds(head * HDIM, HDIM), :] += dot(first_t, ds[head], NN)


def query_kernel(mine, other, out, done):
    done[...] = jnp.zeros_like(done)
    out[...] = ((mine[...] + other[...]) * SCALE).T.astype(out.dtype)


def add_kernel(total, part, out):
    out[...] = (total[...] + part[...].astype(jnp.float32)).astype(out.dtype)


def last_kernel(mine, other, _, grad_keys, grad_values):
    total = mine[...].astype(jnp.float32) + other[...].astype(jnp.float32)
    grad_keys[...] = (total[0] * SCALE).astype(grad_keys.dtype)
    grad_values[...] = total[1].astype(grad_values.dtype)


VM = pl.BlockSpec(memory_space=pltpu.VMEM)
SM = pl.BlockSpec(memory_space=pltpu.SMEM)


BLOCK_COST = pl.CostEstimate(flops=10 * 512 * 512 * 128 // 10, bytes_accessed=2**10, transcendentals=0)
LONG_COST = pl.CostEstimate(flops=40 * 10 * 512 * 512 * 128, bytes_accessed=2**20, transcendentals=0)
NO_COST = pl.CostEstimate(flops=0, bytes_accessed=2**10, transcendentals=0)


def simple(kernel, out, *args, cost=NO_COST):
    return pl.pallas_call(
        kernel,
        out_shape=out,
        in_specs=[VM] * len(args),
        out_specs=jax.tree.map(lambda _: VM, out),
        compiler_params=pltpu.CompilerParams(vmem_limit_bytes=8 * 2**20),
        cost_estimate=cost,
    )(*args)


def call_stats(step, slot, cp, before, kv, rows, groups=(0, 1)):
    size = kv.shape[1]
    out = [jax.ShapeDtypeStruct((6 * len(groups), size), jnp.float32)]
    if step:
        out += [jax.ShapeDtypeStruct((3, 4, size, size), jnp.float32)] * 2
    else:
        out += [jax.ShapeDtypeStruct(a.shape, a.dtype) for a in rows]
    in_specs = [SM] + [VM] * (len(before) + 1 + len(rows))
    if step > 1:
        in_specs[2:4] = [pl.BlockSpec(memory_space=pl.ANY)] * 2
    return pl.pallas_call(
        functools.partial(stats_kernel, step, slot, groups),
        out_shape=out,
        in_specs=in_specs,
        out_specs=[VM] * len(out),
        input_output_aliases={2: 1, 3: 2} if step > 1 else {},
        compiler_params=pltpu.CompilerParams(vmem_limit_bytes=KERNEL_VMEM),
        cost_estimate=NO_COST,
        name="stats",
    )(cp, *before, kv, *rows)


def call_grads(kernel, cp, out, args, cost, scratch=()):
    return pl.pallas_call(
        kernel,
        out_shape=out,
        in_specs=[SM] + [VM] * len(args),
        out_specs=[VM] * len(out),
        scratch_shapes=scratch,
        compiler_params=pltpu.CompilerParams(vmem_limit_bytes=KERNEL_VMEM),
        cost_estimate=cost,
        name="grads",
    )(cp, *args)


def call_first(group, cp, before, rows, kept):
    size = rows[0].shape[0]
    total = (2, size, HDIM)
    out = [jax.ShapeDtypeStruct((2, size, size), jnp.bfloat16), jax.ShapeDtypeStruct((4, size), jnp.float32)]
    out.append(jax.ShapeDtypeStruct(total, jnp.float32 if group else jnp.bfloat16))
    scratch = [] if group else [pltpu.VMEM(total, jnp.float32)]
    args = (*before, rows[group], rows[2 + group], *kept)
    return call_grads(functools.partial(first_kernel, group), cp, out, args, NO_COST if group else BLOCK_COST, scratch)


def call_stage(stage, cp, dq, fin, blocks, rows, kept):
    size = rows[0].shape[0]
    total = (2, size, HDIM)
    out = [jax.ShapeDtypeStruct((2 * HDIM, size), jnp.float32)] * 2
    out.append(jax.ShapeDtypeStruct(total, jnp.float32 if stage == 3 else jnp.bfloat16))
    args = (*dq, *fin, *blocks, *rows[:4], *kept)
    cost = NO_COST if stage == 3 else BLOCK_COST
    *dq, part = call_grads(functools.partial(grads_kernel, stage), cp, out, args, cost, [pltpu.VMEM(total, jnp.float32)])
    return dq, part


def body(query, keys, values, grad_out, doc_start):
    size = query.shape[0]
    position = lax.axis_index("cp").astype(jnp.int32)
    cp = position.reshape(1)
    kv = jnp.where(lax.broadcasted_iota(jnp.int32, (2, *keys.shape), 0) == 0, keys[None], values[None])
    slot1 = chip_shift(kv, 1, 1)
    slot2 = chip_permute(kv, (2, 3, 0, 1), (3, 0, 1, 2))
    slot3 = chip_permute(kv, (3, 0, 1, 2), (2, 3, 0, 1))
    starts = doc_start.reshape(1, size)
    kv, near_query, near_grad = lax.optimization_barrier((kv, query, grad_out))
    far_query, near_starts = lax.optimization_barrier((core_swap(near_query), starts))
    far_grad, far_starts = core_swap(near_grad), core_swap(near_starts)

    stats, *own_rows = call_stats(0, 0, cp, (), kv, (query, grad_out, starts))
    rows = (own_rows[0], far_query, own_rows[1], far_grad, own_rows[2], far_starts)
    before = call_stats(1, 1, cp, (stats, kv), slot1, rows)
    before = call_stats(2, 2, cp, before, slot2, rows)
    stats = before[0]
    near, *kept = call_stats(3, 3, cp, before, slot3, rows, (0,))
    far_other = core_swap(near)
    far, *kept = call_stats(3, 3, cp, (stats, *kept), slot3, rows, (1,))
    near_other = core_swap(far)

    ds_far, fin_far, part = call_first(1, cp, (far, far_other), rows, kept)
    ds_near, fin_near, part = call_first(0, cp, (part, near, near_other), rows, kept)
    back_a = chip_permute(part, (3, 2, 0, 1), (3, 2, 0, 1))
    fin = (fin_near, fin_far)
    dq, part = call_stage(1, cp, (), fin, (slot1, slot2), rows, kept)
    back_b = chip_permute(part, (None, 0, 1, 2), (1, 2, None, 0))
    dq, part = call_stage(2, cp, dq, fin, (slot3, slot1), rows, kept)
    back_c = chip_permute(part, (1, 2, None, 0), (None, 0, 1, 2))
    dq, own = call_stage(3, cp, dq, fin, (kv, kv), rows, (*rows[4:], slot2, slot3, ds_near, ds_far))

    dq_other = core_swap(dq[1])
    token = jax.ShapeDtypeStruct((8, HDIM), jnp.float32)
    grad_query, done = simple(query_kernel, [jax.ShapeDtypeStruct(query.shape, query.dtype), token], dq[0], dq_other)
    total = jax.ShapeDtypeStruct(own.shape, own.dtype)
    half = simple(add_kernel, total, own, back_a, cost=BLOCK_COST)
    half = simple(add_kernel, total, half, back_b, cost=LONG_COST)
    half = simple(add_kernel, jax.ShapeDtypeStruct(kv.shape, kv.dtype), half, back_c)
    other = hd_swap(half)
    near = jax.ShapeDtypeStruct(keys.shape, keys.dtype)
    grad_keys, grad_values = simple(last_kernel, [near] * 2, half, other, done)
    return grad_query, grad_keys, grad_values


def solution(mesh):
    in_specs = (P("cp", "hd"), P("cp", None), P("cp", None), P("cp", "hd"), P("cp"))
    out_specs = (P("cp", "hd"), P("cp", None), P("cp", None))
    return jax.shard_map(body, mesh=mesh, in_specs=in_specs, out_specs=out_specs, check_vma=False)
```
